512 devices in a mesh: rep: 8 (over x, y_lo), shard: 64 (over z, y_hi, core).
Axes of the slice: x: 4, y: 8 (y_hi: 4, y_lo: 2; y = y_hi * 2 + y_lo), z: 8, core: 2. Of those that a mesh axis runs over, the one named last changes fastest.
Arguments:
- activations: bfloat16 [393216, 1024], P(('rep', 'shard')), may hold values from -24 to 24
- cotangents: bfloat16 [393216, 1024], P(('rep', 'shard')), may hold values from -0.0012207031 to 0.0012207031
- statistics: float32 [8, 512, 512], P('rep', 'shard'), may hold values from -22 to 22, as said below
- owner: int32 [8], replicated, may hold values from 0 to 7, each once
Outputs:
- new_statistics: float32 [8, 512, 512], P('rep', 'shard')
- direction: float32 [1024, 1024], P('shard')
The draws below stay inside these ranges and needn't reach their ends.
Inputs may be any that keep to these rules, and one draw needn't show every extreme that they name: `owner`: each root is held by exactly one slot. `statistics`: each slot is symmetric and positive semidefinite.
All inputs are finite; a program needn't handle non-finite values.
Results may differ from the reference program's by a relative error of at most 0.0052.
Values may be sent and summed in bfloat16 or wider, within the bound.
No kernel may reach another device: no remote copies, remote signals or barrier semaphores. Data moves between devices by JAX's collectives and lax.ppermute only.
A program may use at most 64 MiB of HBM per device.

```python
import math
import jax
import jax.numpy as jnp
from jax import lax

B = 512
BLOCK_ROWS = 2
BLOCK_COLS = 2
ITERS = 3
GRAD_ROWS = 1024
GRAD_COLS = 1024
BLOCKS = 4
ROOTS = 8
TOKENS = 393216


def draw_statistics(key, part):
    key = jax.random.fold_in(key, 7)
    column_key, scale_key = jax.random.split(key, 2)
    spread = jnp.exp(jax.random.uniform(scale_key, (ROOTS, B), jnp.float32, 0.0, math.log(10.0)))
    columns = jax.random.truncated_normal(column_key, -2.5, 2.5, (ROOTS, B, 2 * B), jnp.float32)
    mixing = jnp.einsum('rik,rjk->rij', columns, columns, precision=lax.Precision.HIGHEST) / (2.0 * B)
    level = 0.035
    mixing = 0.5 * (mixing + jnp.swapaxes(mixing, 1, 2))
    return level * spread[:, :, None] * mixing * spread[:, None, :]


def with_spikes(values, rng, source, target, blocks, factor):
    owner, partner = [(jnp.arange(values.shape[dim]) // (values.shape[dim] // blocks)).reshape([-1 if axis == dim else 1 for axis in range(values.ndim)]) for dim in (source, target)]
    chosen = jax.random.permutation(rng, blocks)[partner]
    strong = (owner == chosen) | (owner == (partner + blocks // 2) % blocks)
    return jnp.where(strong, factor * values, values)


def steps_of(key, extent, cuts, smallest, high):
    loudness = 1.0
    for axis_at, blocks in cuts:
        steps = jax.random.uniform(jax.random.fold_in(jax.random.fold_in(key, 6), axis_at), (blocks,), jnp.float32, smallest / len(cuts), high / len(cuts))
        loudness = loudness * jnp.repeat(jnp.exp(steps), extent[axis_at] // blocks).reshape((-1,) + (1,) * (len(extent) - 1 - axis_at))
    return loudness


def centred(key, extent, width, limit, shards=(), kind=jnp.bfloat16):
    drawn = jax.random.normal(key, extent, jnp.float32) * width
    if len(shards) > 0:
        drawn = steps_of(key, extent, shards, -0.22, 0.18) * drawn
    return jnp.clip(drawn, min=-limit, max=limit).astype(kind)


def gaussian_with(rng, shape, scale, most, shards, heavy, kind=jnp.bfloat16):
    drawn = scale * jax.random.normal(rng, shape, jnp.float32)
    if shards:
        drawn = drawn * steps_of(rng, shape, shards, -0.22, 0.18)
    return jnp.clip(with_spikes(drawn, jax.random.fold_in(rng, 3), *heavy), -most, most).astype(kind)


def setup_inputs(seed: int = 0) -> dict:
    seeds = jax.random.split(jax.random.key(seed), 5)
    activations = gaussian_with(seeds[0], (TOKENS, GRAD_ROWS), 1.0, 24.0, ((0, 512),), (0, 1, 512, 6.0))
    cotangents = centred(seeds[1], (TOKENS, GRAD_COLS), (64 * TOKENS) ** -0.5, 0.0012207031, ((0, 512),))
    statistics = draw_statistics(jax.random.fold_in(seeds[4], 71), 0)
    owner = jax.random.permutation(seeds[3], ROOTS).astype(jnp.int32)
    return dict(activations=activations, cotangents=cotangents, statistics=statistics, owner=owner)


ema_decay = 0.9
highest = lax.Precision.HIGHEST

def inverse_root(matrix):
    identity = jnp.eye(B, dtype=jnp.float32)
    norm_scale = jnp.sqrt(jnp.sum(matrix * matrix) + 1e-06)
    current = matrix / norm_scale
    result = identity
    for iteration in range(ITERS):
        factor = (5.0 * identity - current) * 0.25
        square = jnp.dot(factor, factor, precision=highest)
        fourth = jnp.dot(square, square, precision=highest)
        current = jnp.dot(fourth, current, precision=highest)
        result = jnp.dot(result, factor, precision=highest)
    return result

def grad_block(gradient, block_id):
    start_row = (block_id // BLOCK_COLS * B).astype(jnp.int32)
    start_col = (block_id % BLOCK_COLS * B).astype(jnp.int32)
    return lax.dynamic_slice(gradient, (start_row, start_col), (B, B))

def reference(activations, cotangents, statistics, owner):
    summed = jnp.dot(activations.T, cotangents, preferred_element_type=jnp.float32)
    gradient = summed.astype(jnp.bfloat16)
    root_ids = jnp.arange(ROOTS, dtype=jnp.int32)
    held_roots = lax.optimization_barrier(jnp.sum(jnp.where(owner[None, :] == root_ids[:, None], root_ids[None, :], 0), axis=1)).astype(jnp.int32)

    def one_slot(inputs):
        slot_stats, root_id = inputs
        grad_tile = grad_block(gradient, root_id % BLOCKS)
        lead_tile = jnp.where(root_id < BLOCKS, grad_tile, grad_tile.T)
        gram_full = jnp.dot(lead_tile, lead_tile.T, preferred_element_type=jnp.float32)
        updated = ema_decay * slot_stats + (1.0 - ema_decay) * gram_full
        return (updated, inverse_root(updated).astype(jnp.bfloat16))
    new_statistics, roots = lax.map(one_slot, (statistics, held_roots))
    rows_out = []
    for block_row in range(BLOCK_ROWS):
        cols_out = []
        for column in range(BLOCK_COLS):
            block_id = block_row * BLOCK_COLS + column
            grad_tile = gradient[block_row * B:(block_row + 1) * B, column * B:(column + 1) * B]
            left_root = roots[owner[block_id]]
            right_root = roots[owner[BLOCKS + block_id]]
            mixed = jnp.dot(left_root, grad_tile, preferred_element_type=jnp.float32).astype(jnp.bfloat16)
            cols_out.append(jnp.dot(mixed, right_root, preferred_element_type=jnp.float32))
        rows_out.append(jnp.concatenate(cols_out, axis=1))
    return (new_statistics, jnp.concatenate(rows_out, axis=0))
```

```python
import functools

import jax
import jax.numpy as jnp
from jax import lax
from jax.experimental import pallas as pl
from jax.experimental.pallas import tpu as pltpu
from jax.sharding import Mesh
from jax.sharding import PartitionSpec as P

ema_decay = 0.9
BLOCK = 512
HALF = BLOCK // 2
QUARTER = BLOCK // 4
LANES = 128
BLOCKS = 4
COLS = 2
REPS = 8
CHIPS = 32
CORES = 2
f32 = jnp.float32
bf16 = jnp.bfloat16
WHOLE = ("chip", "core")
VMEM_LIMIT = 48 * 1024 * 1024


def grad_kernel(owner_ref, core_ref, act_ref, cot_ref, mine_ref, other_ref):
    core = core_ref[0]
    for half in range(2):
        for row in range(2):
            start = row * BLOCK + half * HALF
            act = act_ref[:, start : start + HALF]
            for col in range(COLS):
                cot = cot_ref[:, col * BLOCK : (col + 1) * BLOCK]
                term = lax.dot_general(
                    act, cot, (((0,), (0,)), ((), ())), preferred_element_type=f32
                )
                slot = owner_ref[half * BLOCKS + row * COLS + col]
                low, high = term[:QUARTER], term[QUARTER:]
                mine = jnp.where(core == 0, low, high)
                other = jnp.where(core == 0, high, low)
                for lane in range(BLOCK // LANES):
                    part = slice(lane * LANES, (lane + 1) * LANES)
                    mine_ref[slot, lane] = mine[:, part]
                    other_ref[slot, lane] = other[:, part].astype(other_ref.dtype)


def split(value):
    high = value.astype(bf16)
    return high, (value - high.astype(f32)).astype(bf16)


def product(left, right):
    (lh, ll), (rh, rl) = left, right
    dot = functools.partial(jnp.dot, preferred_element_type=f32)
    return dot(lh, rh) + (dot(lh, rl) + dot(ll, rh))


def root_kernel(place_ref, stats_ref, tiles_ref, updated_ref, root_ref, mixed_ref, grad, full):
    for lane in range(BLOCK // LANES):
        for group in range(QUARTER // 16):
            for core in range(CORES):
                for half in range(2):
                    row = half * HALF + core * QUARTER + group * 16
                    source = (lane * (QUARTER // 16) + group) * CORES + core
                    grad[row : row + 16, lane * LANES : (lane + 1) * LANES] = tiles_ref[source, half]

    @pl.when(place_ref[0] == 1)
    def _left():
        full[...] = lax.dot_general(
            grad[...], grad[...], (((1,), (1,)), ((), ())), preferred_element_type=f32
        )

    @pl.when(place_ref[0] == 0)
    def _right():
        full[...] = lax.dot_general(
            grad[...], grad[...], (((0,), (0,)), ((), ())), preferred_element_type=f32
        )

    updated = ema_decay * stats_ref[...] + (1.0 - ema_decay) * full[...]
    full[...] = updated
    updated_ref[...] = full[pl.ds(pl.multiple_of(place_ref[1], 8), 8), :]
    scale = jnp.sqrt(jnp.sum(updated * updated, keepdims=True) + 1e-06)
    state = updated / scale
    rows = lax.broadcasted_iota(jnp.int32, (BLOCK, BLOCK), 0)
    cols = lax.broadcasted_iota(jnp.int32, (BLOCK, BLOCK), 1)
    five = jnp.where(rows == cols, 1.25, 0.0).astype(f32)

    def step(current):
        factor = split(five - 0.25 * current)
        square = split(product(factor, factor))
        fourth = split(product(square, square))
        return factor, product(fourth, split(current))

    first, state = step(state)
    second, state = step(state)
    third = split(five - 0.25 * state)
    root = product(split(product(first, second)), third)
    root_ref[...] = root.astype(bf16)
    own = root_ref[pl.ds(pl.multiple_of(place_ref[2], 16), 16), :]
    mixed_ref[...] = jnp.dot(own, grad[...], preferred_element_type=f32).astype(bf16)


def exchange(value, axes):
    return lax.all_to_all(value, axes, split_axis=0, concat_axis=0, tiled=True)


def spread(value, axes, count):
    return exchange(jnp.broadcast_to(value[None], (count, *value.shape)), axes)


def pick(table, index):
    return lax.dynamic_index_in_dim(table, index, 0, keepdims=False)


def body(activations, cotangents, statistics, owner):
    replica = lax.axis_index("rep")
    chip = lax.axis_index("chip")
    core = lax.axis_index("core")
    position = chip * CORES + core
    vmem = pl.BlockSpec(memory_space=pltpu.VMEM)
    smem = pl.BlockSpec(memory_space=pltpu.SMEM)
    params = pltpu.CompilerParams(vmem_limit_bytes=VMEM_LIMIT)

    stats = lax.all_gather(statistics[0], WHOLE, axis=0, tiled=True)

    quarter = (REPS, BLOCK // LANES, QUARTER, LANES)
    mine, other = pl.pallas_call(
        grad_kernel,
        out_shape=(jax.ShapeDtypeStruct(quarter, f32), jax.ShapeDtypeStruct(quarter, f32)),
        in_specs=[smem, smem, vmem, vmem],
        out_specs=(vmem, vmem),
        compiler_params=params,
        name="grad_term",
    )(owner, core.reshape(1), activations, cotangents)
    other = lax.ppermute(other, "core", [(0, 1), (1, 0)])
    by_slot = exchange((mine + other).astype(bf16), "rep")
    summed = jnp.sum(by_slot.astype(f32), axis=0).reshape(CHIPS, 16, LANES)
    gradient = jnp.sum(exchange(summed, "chip"), axis=0).astype(bf16)

    roots = jnp.arange(2 * BLOCKS, dtype=jnp.int32)
    held = jnp.sum(jnp.where(owner == replica, roots, 0))
    block = held % BLOCKS
    left_slot, right_slot = pick(owner, block), pick(owner, block + BLOCKS)
    all_slots = spread(gradient, "rep", REPS)
    both = jnp.stack([pick(all_slots, left_slot), pick(all_slots, right_slot)])
    tiles = spread(both, WHOLE, CHIPS * CORES)

    out_rows = 16
    place = jnp.stack(
        [
            (held < BLOCKS).astype(jnp.int32),
            position * 8,
            position % (BLOCK // out_rows) * out_rows,
        ]
    )
    updated, root, mixed = pl.pallas_call(
        root_kernel,
        out_shape=(
            jax.ShapeDtypeStruct((8, BLOCK), f32),
            jax.ShapeDtypeStruct((BLOCK, BLOCK), bf16),
            jax.ShapeDtypeStruct((out_rows, BLOCK), bf16),
        ),
        in_specs=[smem, vmem, vmem],
        out_specs=(vmem, vmem, vmem),
        scratch_shapes=[pltpu.VMEM((BLOCK, BLOCK), bf16), pltpu.VMEM((BLOCK, BLOCK), f32)],
        compiler_params=params,
        name="root",
    )(place, stats, tiles)

    left_rows = pick(spread(mixed, "rep", REPS), left_slot)
    piece = jnp.dot(left_rows, root, preferred_element_type=f32)
    pieces = spread(piece, "rep", REPS)
    first = position // (BLOCK // out_rows) * COLS + BLOCKS
    direction = jnp.concatenate(
        [pick(pieces, pick(owner, first + col)) for col in range(COLS)], axis=1
    )
    return updated[None], direction


def solution(mesh):
    fine = Mesh(mesh.devices.reshape(REPS, CHIPS, CORES), ("rep", "chip", "core"))
    every = ("rep", "chip", "core")
    return jax.shard_map(
        body,
        mesh=fine,
        in_specs=(P(every, None), P(every, None), P("rep", WHOLE, None), P()),
        out_specs=(P("rep", WHOLE, None), P(WHOLE, None)),
        check_vma=False,
    )
```

```python
import jax
import jax.numpy as jnp
from jax import lax
from jax.experimental import pallas as pl
from jax.experimental.pallas import tpu as pltpu
from jax.sharding import Mesh
from jax.sharding import PartitionSpec as P

ema_decay = 0.9
BLOCK = 512
HALF = BLOCK // 2
QUARTER = BLOCK // 4
LANES = 128
BLOCKS = 4
ROOTS = 8
COLS = 2
REPS = 8
CHIPS = 32
CORES = 2
SHARDS = CHIPS * CORES
OUT_ROWS = 16
STATS = 32
f32 = jnp.float32
bf16 = jnp.bfloat16
WHOLE = ("chip", "core")
VMEM_LIMIT = 40 * 1024 * 1024
GRAD_LIMIT = 60 * 1024 * 1024


def slots_of(device, owner_ref):
    replica = device // SHARDS
    held = jnp.int32(0)
    for root in range(1, ROOTS):
        held = jnp.where(owner_ref[root] == replica, root, held)
    block = held % BLOCKS
    return held, owner_ref[block], owner_ref[block + BLOCKS]


def grad_kernel(device_ref, owner_ref, act_hbm, cot_hbm, mine_ref, other_ref, act_ref, cot_ref, sems):
    core = device_ref[0] % CORES

    def fetch(source, target, number, sem):
        columns = pl.ds(number * BLOCK, BLOCK)
        return pltpu.make_async_copy(source.at[:, columns], target.at[:, columns], sems.at[sem])

    act_copies = [fetch(act_hbm, act_ref, row, row) for row in range(2)]
    cot_copies = [fetch(cot_hbm, cot_ref, col, 2 + col) for col in range(2)]
    for copy in (act_copies[0], cot_copies[0], cot_copies[1], act_copies[1]):
        copy.start()
    for row in range(2):
        act_copies[row].wait()
        for col in range(COLS):
            if row == 0:
                cot_copies[col].wait()
            cot = cot_ref[:, col * BLOCK : (col + 1) * BLOCK]
            for half in range(2):
                start = row * BLOCK + half * HALF
                term = lax.dot_general(
                    act_ref[:, start : start + HALF],
                    cot,
                    (((0,), (0,)), ((), ())),
                    preferred_element_type=f32,
                )
                slot = owner_ref[half * BLOCKS + row * COLS + col]
                low, high = term[:QUARTER], term[QUARTER:]
                mine = jnp.where(core == 0, low, high)
                other = jnp.where(core == 0, high, low)
                for lane in range(BLOCK // LANES):
                    part = slice(lane * LANES, (lane + 1) * LANES)
                    mine_ref[slot, lane] = mine[:, part]
                    other_ref[slot, lane] = other[:, part]


def pack_kernel(mine_ref, other_ref, own_ref, out_ref):
    for slot in range(REPS):
        for lane in range(BLOCK // LANES):
            place = slice(lane * QUARTER, (lane + 1) * QUARTER)
            out_ref[slot, place] = (mine_ref[slot, lane] + other_ref[slot, lane]).astype(bf16)
    parts = [own_ref[:, lane * LANES : (lane + 1) * LANES] for lane in range(BLOCK // LANES)]
    packed = jnp.concatenate(parts, axis=0).astype(bf16)
    for slot in range(REPS):
        out_ref[slot, BLOCK : BLOCK + STATS] = packed


def reduce_kernel(device_ref, owner_ref, terms_ref, out_ref):
    _, left, right = slots_of(device_ref[0], owner_ref)
    stats = [terms_ref[slot, BLOCK : BLOCK + STATS] for slot in (left, right)]
    for chip in range(CHIPS):
        part = slice(chip * 16, chip * 16 + 16)
        total = terms_ref[0, part].astype(f32)
        for slot in range(1, REPS):
            total += terms_ref[slot, part].astype(f32)
        high, low = split(total)
        out_ref[chip, 0:16] = high
        out_ref[chip, 16:32] = low
        for side in range(2):
            out_ref[chip, 32 + side * STATS : 32 + (side + 1) * STATS] = stats[side]


def total_kernel(parts_ref, out_ref):
    total = jnp.zeros((16, LANES), f32)
    for chip in range(CHIPS):
        total += parts_ref[chip, 0:16].astype(f32) + parts_ref[chip, 16:32].astype(f32)
    gradient = total.astype(bf16)
    for slot in range(REPS):
        out_ref[slot] = gradient


def pair_kernel(device_ref, owner_ref, slots_ref, out_ref):
    _, left, right = slots_of(device_ref[0], owner_ref)
    first, second = slots_ref[left], slots_ref[right]
    for receiver in range(SHARDS):
        out_ref[receiver, 0] = first
        out_ref[receiver, 1] = second


def split(value):
    high = value.astype(bf16)
    return high, (value - high.astype(f32)).astype(bf16)


def product(left, right):
    return jnp.dot(left.astype(bf16), right.astype(bf16), preferred_element_type=f32)


def newton(stats, gram):
    updated = ema_decay * stats + (1.0 - ema_decay) * gram
    scale = jnp.sqrt(jnp.sum(updated * updated, keepdims=True) + 1e-06)

    def step(state):
        low = 2.0 * state - product(state, state)
        high = 2.0 * low - product(low, low)
        return 1.25**4 * (state - product(high, state))

    first = updated * (0.2 / scale)
    second = step(first)
    return first, second, step(second)


def root_rows(first, second, third, diagonal):
    own_first, own_second, own_third = first
    both = own_first + own_second - product(own_first, second)
    return 1.25**3 * (diagonal - (both + own_third - product(both, third)))


def root_kernel(
    device_ref, owner_ref, own_ref, here_ref, there_ref, tiles_ref, updated_ref, piece_ref, grad, stats, gram, rows
):
    device = device_ref[0]
    held, _, _ = slots_of(device, owner_ref)
    position = device % SHARDS
    core = device % CORES
    for lane in range(BLOCK // LANES):
        for group in range(QUARTER // 16):
            for side in range(CORES):
                for half in range(2):
                    row = half * HALF + side * QUARTER + group * 16
                    source = (lane * (QUARTER // 16) + group) * CORES + side
                    grad[row : row + 16, lane * LANES : (lane + 1) * LANES] = tiles_ref[source, half]
    for chip in range(CHIPS):
        for part, at in ((here_ref, core), (there_ref, 1 - core)):
            place = pl.ds(pl.multiple_of((chip * CORES + at) * 8, 8), 8)
            for side in range(2):
                value = part[chip, 32 + side * STATS : 32 + (side + 1) * STATS].astype(f32)
                for lane in range(BLOCK // LANES):
                    stats[side, place, lane * LANES : (lane + 1) * LANES] = value[lane * 8 : lane * 8 + 8]

    gram[0] = lax.dot_general(
        grad[...], grad[...], (((1,), (1,)), ((), ())), preferred_element_type=f32
    )
    gram[1] = lax.dot_general(
        grad[...], grad[...], (((0,), (0,)), ((), ())), preferred_element_type=f32
    )
    own_gram = gram[held // BLOCKS, pl.ds(pl.multiple_of(position * 8, 8), 8), :]
    updated_ref[...] = ema_decay * own_ref[...] + (1.0 - ema_decay) * own_gram

    start = pl.multiple_of(position % (BLOCK // OUT_ROWS) * OUT_ROWS, OUT_ROWS)
    left = newton(stats[0], gram[0])
    for number in range(3):
        rows[number] = left[number]
    own = tuple(rows[number, pl.ds(start, OUT_ROWS), :] for number in range(3))
    shape = (OUT_ROWS, BLOCK)
    diagonal = lax.broadcasted_iota(jnp.int32, shape, 0) + start == lax.broadcasted_iota(jnp.int32, shape, 1)
    left_rows = root_rows(own, left[1], left[2], jnp.where(diagonal, 1.0, 0.0)).astype(bf16)
    mixed = jnp.dot(left_rows, grad[...], preferred_element_type=f32).astype(bf16)

    right = newton(stats[1], gram[1])
    shape = (BLOCK, BLOCK)
    diagonal = lax.broadcasted_iota(jnp.int32, shape, 0) == lax.broadcasted_iota(jnp.int32, shape, 1)
    right_root = root_rows(right, right[1], right[2], jnp.where(diagonal, 1.0, 0.0)).astype(bf16)
    piece = jnp.dot(mixed, right_root, preferred_element_type=f32)
    for receiver in range(REPS):
        piece_ref[receiver] = piece


def join_kernel(device_ref, owner_ref, pieces_ref, out_ref):
    first = device_ref[0] % SHARDS // (BLOCK // OUT_ROWS) * COLS + BLOCKS
    for col in range(COLS):
        out_ref[:, col * BLOCK : (col + 1) * BLOCK] = pieces_ref[owner_ref[first + col]]


def exchange(value, axes):
    return lax.all_to_all(value, axes, split_axis=0, concat_axis=0, tiled=True)


def call(kernel, name, outs, arrays, scratch=(), limit=VMEM_LIMIT):
    vmem = pl.BlockSpec(memory_space=pltpu.VMEM)
    smem = pl.BlockSpec(memory_space=pltpu.SMEM)
    rest = pl.BlockSpec(memory_space=pl.ANY) if limit > VMEM_LIMIT else vmem
    return pl.pallas_call(
        kernel,
        out_shape=outs,
        in_specs=[smem if array.ndim == 1 else rest for array in arrays],
        out_specs=tuple(vmem for _ in outs) if isinstance(outs, tuple) else vmem,
        scratch_shapes=list(scratch),
        compiler_params=pltpu.CompilerParams(vmem_limit_bytes=limit),
        name=name,
    )(*arrays)


def swap_cores(value):
    return lax.ppermute(value, "core", [(0, 1), (1, 0)])


def body(activations, cotangents, statistics, owner):
    device = lax.axis_index(("rep", "chip", "core")).astype(jnp.int32).reshape(1)
    array = jax.ShapeDtypeStruct
    own = statistics[0]

    quarter = array((REPS, BLOCK // LANES, QUARTER, LANES), f32)
    mine, other = call(
        grad_kernel,
        "grad_term",
        (quarter, quarter),
        (device, owner, activations, cotangents),
        scratch=[
            pltpu.VMEM(activations.shape, bf16),
            pltpu.VMEM(cotangents.shape, bf16),
            pltpu.SemaphoreType.DMA((4,)),
        ],
        limit=GRAD_LIMIT,
    )
    packed = call(
        pack_kernel,
        "pack",
        array((REPS, BLOCK + STATS, LANES), bf16),
        (mine, swap_cores(other), own),
    )
    terms = exchange(packed, "rep")
    reduced = call(
        reduce_kernel,
        "reduce",
        array((CHIPS, 32 + 2 * STATS, LANES), bf16),
        (device, owner, terms),
    )
    here = exchange(reduced, "chip")
    there = swap_cores(here)
    gradient = call(total_kernel, "total", array((REPS, 16, LANES), bf16), (here,))
    both = call(
        pair_kernel,
        "pair",
        array((SHARDS, 2, 16, LANES), bf16),
        (device, owner, exchange(gradient, "rep")),
    )
    tiles = exchange(both, WHOLE)

    updated, pieces = call(
        root_kernel,
        "root",
        (array((8, BLOCK), f32), array((REPS, OUT_ROWS, BLOCK), f32)),
        (device, owner, own, here, there, tiles),
        scratch=[
            pltpu.VMEM((BLOCK, BLOCK), bf16),
            pltpu.VMEM((2, BLOCK, BLOCK), f32),
            pltpu.VMEM((2, BLOCK, BLOCK), f32),
            pltpu.VMEM((3, BLOCK, BLOCK), f32),
        ],
    )
    direction = call(
        join_kernel,
        "join",
        array((OUT_ROWS, COLS * BLOCK), f32),
        (device, owner, exchange(pieces, "rep")),
    )
    return updated[None], direction


def solution(mesh):
    fine = Mesh(mesh.devices.reshape(REPS, CHIPS, CORES), ("rep", "chip", "core"))
    every = ("rep", "chip", "core")
    return jax.shard_map(
        body,
        mesh=fine,
        in_specs=(P(every, None), P(every, None), P("rep", WHOLE, None), P()),
        out_specs=(P("rep", WHOLE, None), P(WHOLE, None)),
        check_vma=False,
    )
```

```python
import functools

import jax
import jax.numpy as jnp
from jax import lax
from jax.experimental import pallas as pl
from jax.experimental.pallas import tpu as pltpu
from jax.sharding import Mesh
from jax.sharding import PartitionSpec as P

ema_decay = 0.9
BLOCK = 512
HALF = BLOCK // 2
GRAD = BLOCK * HALF // 128
LANES = 128
BLOCKS = 4
ROOTS = 8
COLS = 2
XS = 4
YS = 2
CHIPS = 32
CORES = 2
SHARDS = CHIPS * CORES
PARTS = YS * CHIPS
OUT_ROWS = 16
OWN_ROWS = 8
STATS = 32
TILE = 16
f32 = jnp.float32
bf16 = jnp.bfloat16
PLANE = ("yl", "chip")
VMEM_LIMIT = 40 * 1024 * 1024
GRAD_LIMIT = 60 * 1024 * 1024


def held_by(slot, owner_ref):
    held = jnp.int32(0)
    for root in range(1, ROOTS):
        held = jnp.where(owner_ref[root] == slot, root, held)
    return held


def grad_kernel(theirs, device_ref, act_hbm, cot_hbm, out_ref, act_ref, cot_ref, sems):
    core = device_ref[0] % CORES
    half = 1 - core if theirs else core

    def fetch(source, target, number, sem):
        columns = pl.ds(number * BLOCK, BLOCK)
        return pltpu.make_async_copy(source.at[:, columns], target.at[:, columns], sems.at[sem])

    act_copies = [fetch(act_hbm, act_ref, row, row) for row in range(2)]
    cot_copies = [fetch(cot_hbm, cot_ref, col, 2 + col) for col in range(COLS)]
    for copy in (act_copies[0], cot_copies[0], cot_copies[1], act_copies[1]):
        copy.start()
    for row in range(2):
        act_copies[row].wait()
        start = pl.multiple_of(row * BLOCK + half * HALF, HALF)
        act = act_ref[:, pl.ds(start, HALF)]
        for col in range(COLS):
            if row == 0:
                cot_copies[col].wait()
            term = lax.dot_general(
                act,
                cot_ref[:, col * BLOCK : (col + 1) * BLOCK],
                (((0,), (0,)), ((), ())),
                preferred_element_type=f32,
            ).astype(out_ref.dtype)
            for lane in range(BLOCK // LANES):
                out_ref[row * COLS + col, lane] = term[:, lane * LANES : (lane + 1) * LANES]


def stats_kernel(own_ref, out_ref):
    parts = [own_ref[:, lane * LANES : (lane + 1) * LANES] for lane in range(BLOCK // LANES)]
    out_ref[...] = jnp.concatenate(parts, axis=0).astype(bf16)


def pack_kernel(mine_ref, other_ref, own_ref, next_ref, out_ref):
    for block in range(BLOCKS):
        for lane in range(BLOCK // LANES):
            place = slice(lane * HALF, (lane + 1) * HALF)
            total = mine_ref[block, lane] + other_ref[block, lane].astype(f32)
            out_ref[block, place] = total.astype(bf16)
        out_ref[block, GRAD : GRAD + STATS] = own_ref[...]
        out_ref[block, GRAD + STATS : GRAD + 2 * STATS] = next_ref[...]


def reduce_kernel(device_ref, owner_ref, terms_ref, out_ref):
    replica = device_ref[0] // SHARDS
    block, side = replica // YS, replica % YS
    slot = owner_ref[side * BLOCKS + block]
    place = pl.multiple_of(GRAD + jnp.where(slot % YS == side, 0, STATS), STATS)
    stats = terms_ref[slot // YS, pl.ds(place, STATS)]
    for part in range(PARTS):
        rows = slice(part * TILE, (part + 1) * TILE)
        total = terms_ref[0, rows].astype(f32)
        for source in range(1, XS):
            total += terms_ref[source, rows].astype(f32)
        out_ref[part, :TILE] = total.astype(bf16)
        out_ref[part, TILE:] = stats


def total_kernel(parts_ref, gradient_ref, stats_ref):
    total = parts_ref[0, :TILE].astype(f32)
    for part in range(1, PARTS):
        total += parts_ref[part, :TILE].astype(f32)
    gradient = total.astype(bf16)
    for part in range(PARTS):
        gradient_ref[part] = gradient
        stats_ref[part] = parts_ref[part, TILE:]


def product(left, right):
    return jnp.dot(left.astype(bf16), right.astype(bf16), preferred_element_type=f32)


def newton(stats, gram):
    updated = ema_decay * stats + (1.0 - ema_decay) * gram
    scale = jnp.sqrt(jnp.sum(updated * updated, keepdims=True) + 1e-06)

    def step(state):
        low = 2.0 * state - product(state, state)
        high = 2.0 * low - product(low, low)
        return 1.25**4 * (state - product(high, state))

    first = updated * (0.2 / scale)
    second = step(first)
    return first, second, step(second)


def root_rows(first, second, third, diagonal):
    own_first, own_second, own_third = first
    both = own_first + own_second - product(own_first, second)
    return 1.25**3 * (diagonal - (both + own_third - product(both, third)))


def root_kernel(
    device_ref,
    owner_ref,
    stats_here_ref,
    stats_there_ref,
    tiles_here_ref,
    tiles_there_ref,
    out_ref,
    grad,
    stats,
    gram,
    rows,
):
    device = device_ref[0]
    replica = device // SHARDS
    position = device % SHARDS
    core = device % CORES
    for tiles_ref, at in ((tiles_here_ref, core), (tiles_there_ref, 1 - core)):
        for part in range(PARTS):
            lane, group = divmod(part, HALF // TILE)
            place = pl.ds(pl.multiple_of(at * HALF + group * TILE, TILE), TILE)
            grad[place, lane * LANES : (lane + 1) * LANES] = tiles_ref[part]
    for stats_ref, at in ((stats_here_ref, core), (stats_there_ref, 1 - core)):
        for side in range(2):
            for chip in range(CHIPS):
                value = stats_ref[side * CHIPS + chip].astype(f32)
                place = pl.ds(pl.multiple_of((chip * CORES + at) * 8, 8), 8)
                for lane in range(BLOCK // LANES):
                    stats[side, place, lane * LANES : (lane + 1) * LANES] = value[lane * 8 : lane * 8 + 8]

    gram[0] = lax.dot_general(
        grad[...], grad[...], (((1,), (1,)), ((), ())), preferred_element_type=f32
    )
    gram[1] = lax.dot_general(
        grad[...], grad[...], (((0,), (0,)), ((), ())), preferred_element_type=f32
    )
    own = pl.ds(pl.multiple_of(position * OWN_ROWS, OWN_ROWS), OWN_ROWS)
    for receiver in range(XS):
        held = held_by(receiver * YS + replica % YS, owner_ref)
        out_ref[receiver, OUT_ROWS:] = gram[held // BLOCKS, own, :]

    start = pl.multiple_of(position % (BLOCK // OUT_ROWS) * OUT_ROWS, OUT_ROWS)
    left = newton(stats[0], gram[0])
    for number in range(3):
        rows[number] = left[number]
    own = tuple(rows[number, pl.ds(start, OUT_ROWS), :] for number in range(3))
    shape = (OUT_ROWS, BLOCK)
    diagonal = lax.broadcasted_iota(jnp.int32, shape, 0) + start == lax.broadcasted_iota(jnp.int32, shape, 1)
    left_rows = root_rows(own, left[1], left[2], jnp.where(diagonal, 1.0, 0.0)).astype(bf16)
    mixed = jnp.dot(left_rows, grad[...], preferred_element_type=f32).astype(bf16)

    right = newton(stats[1], gram[1])
    shape = (BLOCK, BLOCK)
    diagonal = lax.broadcasted_iota(jnp.int32, shape, 0) == lax.broadcasted_iota(jnp.int32, shape, 1)
    right_root = root_rows(right, right[1], right[2], jnp.where(diagonal, 1.0, 0.0)).astype(bf16)
    piece = jnp.dot(mixed, right_root, preferred_element_type=f32)
    for receiver in range(XS):
        out_ref[receiver, :OUT_ROWS] = piece


def join_kernel(device_ref, owner_ref, own_ref, pieces_ref, updated_ref, direction_ref):
    device = device_ref[0]
    block = held_by(device // SHARDS, owner_ref) % BLOCKS
    updated_ref[...] = ema_decay * own_ref[...] + (1.0 - ema_decay) * pieces_ref[block, OUT_ROWS:]
    first = device % SHARDS // (BLOCK // OUT_ROWS) * COLS
    for col in range(COLS):
        direction_ref[:, col * BLOCK : (col + 1) * BLOCK] = pieces_ref[first + col, :OUT_ROWS]


def exchange(value, axes):
    return lax.all_to_all(value, axes, split_axis=0, concat_axis=0, tiled=True)


def call(kernel, name, outs, arrays, scratch=(), limit=VMEM_LIMIT):
    vmem = pl.BlockSpec(memory_space=pltpu.VMEM)
    smem = pl.BlockSpec(memory_space=pltpu.SMEM)
    rest = pl.BlockSpec(memory_space=pl.ANY) if limit > VMEM_LIMIT else vmem
    return pl.pallas_call(
        kernel,
        out_shape=outs,
        in_specs=[smem if array.ndim == 1 else rest for array in arrays],
        out_specs=tuple(vmem for _ in outs) if isinstance(outs, tuple) else vmem,
        scratch_shapes=list(scratch),
        compiler_params=pltpu.CompilerParams(vmem_limit_bytes=limit),
        name=name,
    )(*arrays)


def swap(value, axis):
    return lax.ppermute(value, axis, [(0, 1), (1, 0)])


def body(activations, cotangents, statistics, owner):
    device = lax.axis_index(("x", "yl", "chip", "core")).astype(jnp.int32).reshape(1)
    array = jax.ShapeDtypeStruct
    own = statistics[0]

    def gradient_half(theirs, kind):
        return call(
            functools.partial(grad_kernel, theirs),
            "grad_theirs" if theirs else "grad_mine",
            array((BLOCKS, BLOCK // LANES, HALF, LANES), kind),
            (device, activations, cotangents),
            scratch=[
                pltpu.VMEM(activations.shape, bf16),
                pltpu.VMEM(cotangents.shape, bf16),
                pltpu.SemaphoreType.DMA((4,)),
            ],
            limit=GRAD_LIMIT,
        )

    own_stats = call(stats_kernel, "stats", array((STATS, LANES), bf16), (own,))
    next_stats = swap(own_stats, "yl")
    other = swap(gradient_half(True, bf16), "core")
    mine = gradient_half(False, f32)
    packed = call(
        pack_kernel,
        "pack",
        array((XS, GRAD + 2 * STATS, LANES), bf16),
        (mine, other, own_stats, next_stats),
    )
    terms = exchange(packed, "x")
    reduced = call(
        reduce_kernel,
        "reduce",
        array((PARTS, TILE + STATS, LANES), bf16),
        (device, owner, terms),
    )
    gradient, stats = call(
        total_kernel,
        "total",
        (array((PARTS, TILE, LANES), bf16), array((PARTS, STATS, LANES), bf16)),
        (exchange(reduced, PLANE),),
    )
    tiles = exchange(gradient, PLANE)
    pieces = call(
        root_kernel,
        "root",
        array((XS, OUT_ROWS + OWN_ROWS, BLOCK), f32),
        (device, owner, stats, swap(stats, "core"), tiles, swap(tiles, "core")),
        scratch=[
            pltpu.VMEM((BLOCK, BLOCK), bf16),
            pltpu.VMEM((2, BLOCK, BLOCK), f32),
            pltpu.VMEM((2, BLOCK, BLOCK), f32),
            pltpu.VMEM((3, BLOCK, BLOCK), f32),
        ],
    )
    updated, direction = call(
        join_kernel,
        "join",
        (array((OWN_ROWS, BLOCK), f32), array((OUT_ROWS, COLS * BLOCK), f32)),
        (device, owner, own, exchange(pieces, "x")),
    )
    return updated[None], direction


def solution(mesh):
    fine = Mesh(mesh.devices.reshape(XS, YS, CHIPS, CORES), ("x", "yl", "chip", "core"))
    rep, shard = ("x", "yl"), ("chip", "core")
    every = rep + shard
    return jax.shard_map(
        body,
        mesh=fine,
        in_specs=(P(every, None), P(every, None), P(rep, shard, None), P()),
        out_specs=(P(rep, shard, None), P(shard, None)),
        check_vma=False,
    )
```

```python
import jax
import jax.numpy as jnp
from jax import lax
from jax.experimental import pallas as pl
from jax.experimental.pallas import tpu as pltpu
from jax.sharding import Mesh
from jax.sharding import PartitionSpec as P

ema_decay = 0.9
BLOCK = 512
HALF = BLOCK // 2
LANES = 128
BLOCKS = 4
ROOTS = 8
COLS = 2
XS = 4
PAIR = 2
CORES = 2
SHARDS = 64
QUADS = 4
FAR = 16
PARTS = QUADS * FAR
OUT_ROWS = 16
OWN_ROWS = 8
STATS = 32
TILE = 16
f32 = jnp.float32
bf16 = jnp.bfloat16
NEAR_AXES = ("x", "yl", "zp")
FAR_AXES = ("z4", "yh")
PLANE = ("yl", "zp") + FAR_AXES
VMEM_LIMIT = 40 * 1024 * 1024
GRAD_LIMIT = 60 * 1024 * 1024


def held_by(slot, owner_ref):
    held = jnp.int32(0)
    for root in range(1, ROOTS):
        held = jnp.where(owner_ref[root] == slot, root, held)
    return held


def near_place(device):
    return device // (PAIR * SHARDS), device // SHARDS % PAIR, device // 8 % PAIR, device % CORES


def theirs_kernel(device_ref, act_hbm, cot_hbm, out_ref, act_ref, cot_ref, sems):
    half = 1 - device_ref[0] % CORES
    copies = []
    for row in range(2):
        start = pl.multiple_of(row * BLOCK + half * HALF, HALF)
        copies.append(
            pltpu.make_async_copy(act_hbm.at[:, pl.ds(start, HALF)], act_ref.at[row], sems.at[row])
        )
    for col in range(COLS):
        columns = pl.ds(col * BLOCK, BLOCK)
        copies.append(
            pltpu.make_async_copy(cot_hbm.at[:, columns], cot_ref.at[col], sems.at[2 + col])
        )
    for number in (0, 2, 3, 1):
        copies[number].start()
    for row in range(2):
        copies[row].wait()
        for col in range(COLS):
            if row == 0:
                copies[2 + col].wait()
            term = half_term(act_ref[row], cot_ref[col]).astype(bf16)
            for lane in range(QUADS):
                out_ref[row * COLS + col, lane] = term[:, lane * LANES : (lane + 1) * LANES]


def half_term(act, cot):
    return lax.dot_general(act, cot, (((0,), (0,)), ((), ())), preferred_element_type=f32)


def mine_kernel(device_ref, act_ref, cot_ref, other_ref, own_ref, out_ref):
    half = device_ref[0] % CORES
    parts = [own_ref[:, lane * LANES : (lane + 1) * LANES] for lane in range(BLOCK // LANES)]
    stats = jnp.concatenate(parts, axis=0).astype(bf16)
    for row in range(2):
        start = pl.multiple_of(row * BLOCK + half * HALF, HALF)
        act = act_ref[:, pl.ds(start, HALF)]
        for col in range(COLS):
            block = row * COLS + col
            term = half_term(act, cot_ref[:, col * BLOCK : (col + 1) * BLOCK])
            for lane in range(QUADS):
                total = term[:, lane * LANES : (lane + 1) * LANES] + other_ref[block, lane].astype(f32)
                out_ref[block * QUADS + lane, :HALF] = total.astype(bf16)
                out_ref[block * QUADS + lane, HALF:] = stats


def reduce_kernel(device_ref, owner_ref, terms_ref, out_ref):
    block, side, low, _ = near_place(device_ref[0])
    stats = terms_ref[owner_ref[side * BLOCKS + block] * PAIR + low, HALF:]
    for part in range(FAR):
        rows = slice(part * TILE, (part + 1) * TILE)
        total = terms_ref[0, rows].astype(f32)
        for source in range(1, XS * QUADS):
            total += terms_ref[source, rows].astype(f32)
        out_ref[part, :TILE] = total.astype(bf16)
        out_ref[part, TILE:] = stats


def total_kernel(parts_ref, gradient_ref, stats_ref):
    total = parts_ref[0, :TILE].astype(f32)
    for part in range(1, FAR):
        total += parts_ref[part, :TILE].astype(f32)
    gradient = total.astype(bf16)
    for part in range(PARTS):
        gradient_ref[part] = gradient
    for part in range(FAR):
        stats_ref[part] = parts_ref[part, TILE:]


def product(left, right):
    return jnp.dot(left.astype(bf16), right.astype(bf16), preferred_element_type=f32)


def newton(stats, gram):
    updated = ema_decay * stats + (1.0 - ema_decay) * gram
    scale = jnp.sqrt(jnp.sum(updated * updated, keepdims=True) + 1e-06)

    def step(state):
        low = 2.0 * state - product(state, state)
        high = 2.0 * low - product(low, low)
        return 1.25**4 * (state - product(high, state))

    first = updated * (0.2 / scale)
    second = step(first)
    return first, second, step(second)


def root_rows(first, second, third, diagonal):
    own_first, own_second, own_third = first
    both = own_first + own_second - product(own_first, second)
    return 1.25**3 * (diagonal - (both + own_third - product(both, third)))


def root_kernel(
    device_ref,
    owner_ref,
    stats_here_ref,
    stats_there_ref,
    tiles_here_ref,
    tiles_there_ref,
    out_ref,
    grad,
    stats,
    gram,
    rows,
):
    device = device_ref[0]
    position = device % SHARDS
    _, near_y, near_z, core = near_place(device)
    for tiles_ref, at in ((tiles_here_ref, core), (tiles_there_ref, 1 - core)):
        for part in range(PARTS):
            lane, group = divmod(part, FAR)
            place = pl.ds(pl.multiple_of(at * HALF + group * TILE, TILE), TILE)
            grad[place, lane * LANES : (lane + 1) * LANES] = tiles_ref[part]
    for stats_ref, at in ((stats_here_ref, core), (stats_there_ref, 1 - core)):
        for quad in range(QUADS):
            side = near_y if quad // PAIR == 0 else 1 - near_y
            low = near_z if quad % PAIR == 0 else 1 - near_z
            for part in range(FAR):
                high, column = divmod(part, 4)
                value = stats_ref[quad, part].astype(f32)
                shard = (high * PAIR + low) * 8 + column * CORES + at
                place = pl.ds(pl.multiple_of(shard * OWN_ROWS, OWN_ROWS), OWN_ROWS)
                for lane in range(BLOCK // LANES):
                    columns = slice(lane * LANES, (lane + 1) * LANES)
                    stats[side, place, columns] = value[lane * OWN_ROWS : (lane + 1) * OWN_ROWS]

    gram[0] = lax.dot_general(
        grad[...], grad[...], (((1,), (1,)), ((), ())), preferred_element_type=f32
    )
    gram[1] = lax.dot_general(
        grad[...], grad[...], (((0,), (0,)), ((), ())), preferred_element_type=f32
    )
    own = pl.ds(pl.multiple_of(position * OWN_ROWS, OWN_ROWS), OWN_ROWS)
    for receiver in range(XS):
        held = held_by(receiver * PAIR + near_y, owner_ref)
        out_ref[receiver, OUT_ROWS:] = gram[held // BLOCKS, own, :]

    start = pl.multiple_of(position % (BLOCK // OUT_ROWS) * OUT_ROWS, OUT_ROWS)
    left = newton(stats[0], gram[0])
    for number in range(3):
        rows[number] = left[number]
    own = tuple(rows[number, pl.ds(start, OUT_ROWS), :] for number in range(3))
    shape = (OUT_ROWS, BLOCK)
    diagonal = lax.broadcasted_iota(jnp.int32, shape, 0) + start == lax.broadcasted_iota(jnp.int32, shape, 1)
    left_rows = root_rows(own, left[1], left[2], jnp.where(diagonal, 1.0, 0.0)).astype(bf16)
    mixed = jnp.dot(left_rows, grad[...], preferred_element_type=f32).astype(bf16)

    right = newton(stats[1], gram[1])
    shape = (BLOCK, BLOCK)
    diagonal = lax.broadcasted_iota(jnp.int32, shape, 0) == lax.broadcasted_iota(jnp.int32, shape, 1)
    right_root = root_rows(right, right[1], right[2], jnp.where(diagonal, 1.0, 0.0)).astype(bf16)
    piece = jnp.dot(mixed, right_root, preferred_element_type=f32)
    for receiver in range(XS):
        out_ref[receiver, :OUT_ROWS] = piece


def join_kernel(device_ref, owner_ref, own_ref, pieces_ref, updated_ref, direction_ref):
    device = device_ref[0]
    block = held_by(device // SHARDS, owner_ref) % BLOCKS
    updated_ref[...] = ema_decay * own_ref[...] + (1.0 - ema_decay) * pieces_ref[block, OUT_ROWS:]
    first = device % SHARDS // (BLOCK // OUT_ROWS) * COLS
    for col in range(COLS):
        direction_ref[:, col * BLOCK : (col + 1) * BLOCK] = pieces_ref[first + col, :OUT_ROWS]


def exchange(value, axes):
    return lax.all_to_all(value, axes, split_axis=0, concat_axis=0, tiled=True)


def call(kernel, name, outs, arrays, scratch=(), limit=VMEM_LIMIT):
    vmem = pl.BlockSpec(memory_space=pltpu.VMEM)
    smem = pl.BlockSpec(memory_space=pltpu.SMEM)
    rest = pl.BlockSpec(memory_space=pl.ANY) if limit > VMEM_LIMIT else vmem
    return pl.pallas_call(
        kernel,
        out_shape=outs,
        in_specs=[smem if array.ndim == 1 else rest for array in arrays],
        out_specs=tuple(vmem for _ in outs) if isinstance(outs, tuple) else vmem,
        scratch_shapes=list(scratch),
        compiler_params=pltpu.CompilerParams(vmem_limit_bytes=limit),
        name=name,
    )(*arrays)


def swap(value, axis):
    return lax.ppermute(value, axis, [(0, 1), (1, 0)])


def swap_near(value):
    both = [(place, 3 - place) for place in range(QUADS)]
    return jnp.stack(
        [value, swap(value, "zp"), swap(value, "yl"), lax.ppermute(value, ("yl", "zp"), both)]
    )


def body(activations, cotangents, statistics, owner):
    device = lax.axis_index(("x", "yl", "z4", "zp", "yh", "core")).astype(jnp.int32).reshape(1)
    array = jax.ShapeDtypeStruct
    own = statistics[0]
    tokens = activations.shape[0]

    other = call(
        theirs_kernel,
        "grad_theirs",
        array((BLOCKS, QUADS, HALF, LANES), bf16),
        (device, activations, cotangents),
        scratch=[
            pltpu.VMEM((2, tokens, HALF), bf16),
            pltpu.VMEM((COLS, tokens, BLOCK), bf16),
            pltpu.SemaphoreType.DMA((4,)),
        ],
        limit=GRAD_LIMIT,
    )
    packed = call(
        mine_kernel,
        "grad_mine",
        array((XS * QUADS, HALF + STATS, LANES), bf16),
        (device, activations, cotangents, swap(other, "core"), own),
    )
    reduced = call(
        reduce_kernel,
        "reduce",
        array((FAR, TILE + STATS, LANES), bf16),
        (device, owner, exchange(packed, NEAR_AXES)),
    )
    gradient, stats = call(
        total_kernel,
        "total",
        (array((PARTS, TILE, LANES), bf16), array((FAR, STATS, LANES), bf16)),
        (exchange(reduced, FAR_AXES),),
    )
    stats = swap_near(stats)
    tiles = exchange(gradient, PLANE)
    pieces = call(
        root_kernel,
        "root",
        array((XS, OUT_ROWS + OWN_ROWS, BLOCK), f32),
        (device, owner, stats, swap(stats, "core"), tiles, swap(tiles, "core")),
        scratch=[
            pltpu.VMEM((BLOCK, BLOCK), bf16),
            pltpu.VMEM((2, BLOCK, BLOCK), f32),
            pltpu.VMEM((2, BLOCK, BLOCK), f32),
            pltpu.VMEM((3, BLOCK, BLOCK), f32),
        ],
    )
    updated, direction = call(
        join_kernel,
        "join",
        (array((OWN_ROWS, BLOCK), f32), array((OUT_ROWS, COLS * BLOCK), f32)),
        (device, owner, own, exchange(pieces, "x")),
    )
    return updated[None], direction


def solution(mesh):
    sizes = {"x": 4, "yl": 2, "z4": 4, "zp": 2, "yh": 4, "core": 2}
    fine = Mesh(mesh.devices.reshape(tuple(sizes.values())), tuple(sizes))
    every = tuple(sizes)
    rep, shard = every[:2], every[2:]
    return jax.shard_map(
        body,
        mesh=fine,
        in_specs=(P(every, None), P(every, None), P(rep, shard, None), P()),
        out_specs=(P(rep, shard, None), P(shard, None)),
        check_vma=False,
    )
```

```python
import jax
import jax.numpy as jnp
from jax import lax
from jax.experimental import pallas as pl
from jax.experimental.pallas import tpu as pltpu
from jax.sharding import Mesh
from jax.sharding import PartitionSpec as P

ema_decay = 0.9
BLOCK = 512
HALF = BLOCK // 2
LANES = 128
BLOCKS = 4
ROOTS = 8
COLS = 2
XS = 4
PAIR = 2
CORES = 2
SHARDS = 64
QUADS = 4
FAR = 16
PARTS = QUADS * FAR
OUT_ROWS = 16
OWN_ROWS = 8
STATS = 32
TILE = 16
f32 = jnp.float32
bf16 = jnp.bfloat16
NEAR_AXES = ("x", "yl", "zp")
FAR_AXES = ("z4", "yh")
PLANE = ("yl", "zp") + FAR_AXES
VMEM_LIMIT = 40 * 1024 * 1024
GRAD_LIMIT = 60 * 1024 * 1024


def held_by(slot, owner_ref):
    held = jnp.int32(0)
    for root in range(1, ROOTS):
        held = jnp.where(owner_ref[root] == slot, root, held)
    return held


def near_place(device):
    return device // (PAIR * SHARDS), device // SHARDS % PAIR, device // 8 % PAIR, device % CORES


def theirs_kernel(device_ref, act_hbm, cot_hbm, out_ref, act_ref, cot_ref, sems):
    half = 1 - device_ref[0] % CORES
    copies = []
    for row in range(2):
        start = pl.multiple_of(row * BLOCK + half * HALF, HALF)
        copies.append(
            pltpu.make_async_copy(act_hbm.at[:, pl.ds(start, HALF)], act_ref.at[row], sems.at[row])
        )
    for col in range(COLS):
        columns = pl.ds(col * BLOCK, BLOCK)
        copies.append(
            pltpu.make_async_copy(cot_hbm.at[:, columns], cot_ref.at[col], sems.at[2 + col])
        )
    for number in (0, 2, 3, 1):
        copies[number].start()
    for row in range(2):
        copies[row].wait()
        for col in range(COLS):
            if row == 0:
                copies[2 + col].wait()
            term = half_term(act_ref[row], cot_ref[col]).astype(bf16)
            for lane in range(QUADS):
                out_ref[row * COLS + col, lane] = term[:, lane * LANES : (lane + 1) * LANES]


def half_term(act, cot):
    return lax.dot_general(act, cot, (((0,), (0,)), ((), ())), preferred_element_type=f32)


def mine_kernel(device_ref, act_ref, cot_ref, other_ref, own_ref, out_ref):
    half = device_ref[0] % CORES
    parts = [own_ref[:, lane * LANES : (lane + 1) * LANES] for lane in range(BLOCK // LANES)]
    stats = jnp.concatenate(parts, axis=0).astype(bf16)
    for row in range(2):
        start = pl.multiple_of(row * BLOCK + half * HALF, HALF)
        act = act_ref[:, pl.ds(start, HALF)]
        for col in range(COLS):
            block = row * COLS + col
            term = half_term(act, cot_ref[:, col * BLOCK : (col + 1) * BLOCK])
            for lane in range(QUADS):
                total = term[:, lane * LANES : (lane + 1) * LANES] + other_ref[block, lane].astype(f32)
                out_ref[block * QUADS + lane, :HALF] = total.astype(bf16)
                out_ref[block * QUADS + lane, HALF:] = stats


def reduce_kernel(device_ref, owner_ref, terms_ref, out_ref):
    block, side, _, _ = near_place(device_ref[0])
    first = owner_ref[side * BLOCKS + block] * PAIR
    stats = [terms_ref[first + low, HALF:] for low in range(PAIR)]
    for part in range(FAR):
        rows = slice(part * TILE, (part + 1) * TILE)
        total = terms_ref[0, rows].astype(f32)
        for source in range(1, XS * QUADS):
            total += terms_ref[source, rows].astype(f32)
        out_ref[part, :TILE] = total.astype(bf16)
        for low in range(PAIR):
            out_ref[part, TILE + low * STATS : TILE + (low + 1) * STATS] = stats[low]


def total_kernel(parts_ref, gradient_ref, stats_ref):
    total = parts_ref[0, :TILE].astype(f32)
    for part in range(1, FAR):
        total += parts_ref[part, :TILE].astype(f32)
    gradient = total.astype(bf16)
    for part in range(PARTS):
        gradient_ref[part] = gradient
    for part in range(FAR):
        for low in range(PAIR):
            place = slice(TILE + low * STATS, TILE + (low + 1) * STATS)
            stats_ref[low, part] = parts_ref[part, place]


def unpack_kernel(device_ref, stats_here_ref, stats_there_ref, stats):
    _, near_y, _, core = near_place(device_ref[0])
    for stats_ref, at in ((stats_here_ref, core), (stats_there_ref, 1 - core)):
        for quad in range(QUADS):
            side = near_y if quad // PAIR == 0 else 1 - near_y
            low = quad % PAIR
            for part in range(FAR):
                high, column = divmod(part, 4)
                value = stats_ref[quad, part].astype(f32)
                shard = (high * PAIR + low) * 8 + column * CORES + at
                place = pl.ds(pl.multiple_of(shard * OWN_ROWS, OWN_ROWS), OWN_ROWS)
                for lane in range(BLOCK // LANES):
                    columns = slice(lane * LANES, (lane + 1) * LANES)
                    stats[side, place, columns] = value[lane * OWN_ROWS : (lane + 1) * OWN_ROWS]

def product(left, right):
    return jnp.dot(left.astype(bf16), right.astype(bf16), preferred_element_type=f32)


def newton(stats, gram):
    sides = range(2)
    updated = [ema_decay * stats[side] + (1.0 - ema_decay) * gram[side] for side in sides]
    scales = [jnp.sqrt(jnp.sum(value * value, keepdims=True) + 1e-06) for value in updated]

    def step(state):
        low = [2.0 * state[side] - product(state[side], state[side]) for side in sides]
        high = [2.0 * low[side] - product(low[side], low[side]) for side in sides]
        return [1.25**4 * (state[side] - product(high[side], state[side])) for side in sides]

    first = [updated[side] * (0.2 / scales[side]) for side in sides]
    second = step(first)
    return first, second, step(second)


def root_rows(first, second, third, diagonal):
    own_first, own_second, own_third = first
    both = own_first + own_second - product(own_first, second)
    return 1.25**3 * (diagonal - (both + own_third - product(both, third)))


def root_kernel(
    device_ref,
    owner_ref,
    stats,
    tiles_here_ref,
    tiles_there_ref,
    out_ref,
    grad,
    gram,
    rows,
):
    device = device_ref[0]
    position = device % SHARDS
    _, near_y, _, core = near_place(device)
    for tiles_ref, at in ((tiles_here_ref, core), (tiles_there_ref, 1 - core)):
        for part in range(PARTS):
            lane, group = divmod(part, FAR)
            place = pl.ds(pl.multiple_of(at * HALF + group * TILE, TILE), TILE)
            grad[place, lane * LANES : (lane + 1) * LANES] = tiles_ref[part]
    gram[0] = lax.dot_general(
        grad[...], grad[...], (((1,), (1,)), ((), ())), preferred_element_type=f32
    )
    gram[1] = lax.dot_general(
        grad[...], grad[...], (((0,), (0,)), ((), ())), preferred_element_type=f32
    )
    own = pl.ds(pl.multiple_of(position * OWN_ROWS, OWN_ROWS), OWN_ROWS)
    for receiver in range(XS):
        held = held_by(receiver * PAIR + near_y, owner_ref)
        out_ref[receiver, OUT_ROWS:] = gram[held // BLOCKS, own, :]

    start = pl.multiple_of(position % (BLOCK // OUT_ROWS) * OUT_ROWS, OUT_ROWS)
    states = newton(stats, gram)
    left, right = [[state[side] for state in states] for side in range(2)]
    for number in range(3):
        rows[number] = left[number]
    own = tuple(rows[number, pl.ds(start, OUT_ROWS), :] for number in range(3))
    shape = (OUT_ROWS, BLOCK)
    diagonal = lax.broadcasted_iota(jnp.int32, shape, 0) + start == lax.broadcasted_iota(jnp.int32, shape, 1)
    left_rows = root_rows(own, left[1], left[2], jnp.where(diagonal, 1.0, 0.0)).astype(bf16)
    mixed = jnp.dot(left_rows, grad[...], preferred_element_type=f32).astype(bf16)

    shape = (BLOCK, BLOCK)
    diagonal = lax.broadcasted_iota(jnp.int32, shape, 0) == lax.broadcasted_iota(jnp.int32, shape, 1)
    right_root = root_rows(right, right[1], right[2], jnp.where(diagonal, 1.0, 0.0)).astype(bf16)
    piece = jnp.dot(mixed, right_root, preferred_element_type=f32)
    for receiver in range(XS):
        out_ref[receiver, :OUT_ROWS] = piece


def join_kernel(device_ref, owner_ref, own_ref, pieces_ref, updated_ref, direction_ref):
    device = device_ref[0]
    block = held_by(device // SHARDS, owner_ref) % BLOCKS
    updated_ref[...] = ema_decay * own_ref[...] + (1.0 - ema_decay) * pieces_ref[block, OUT_ROWS:]
    first = device % SHARDS // (BLOCK // OUT_ROWS) * COLS
    for col in range(COLS):
        direction_ref[:, col * BLOCK : (col + 1) * BLOCK] = pieces_ref[first + col, :OUT_ROWS]


def exchange(value, axes):
    return lax.all_to_all(value, axes, split_axis=0, concat_axis=0, tiled=True)


def call(kernel, name, outs, arrays, scratch=(), limit=VMEM_LIMIT):
    vmem = pl.BlockSpec(memory_space=pltpu.VMEM)
    smem = pl.BlockSpec(memory_space=pltpu.SMEM)
    rest = pl.BlockSpec(memory_space=pl.ANY) if limit > VMEM_LIMIT else vmem
    return pl.pallas_call(
        kernel,
        out_shape=outs,
        in_specs=[smem if array.ndim == 1 else rest for array in arrays],
        out_specs=tuple(vmem for _ in outs) if isinstance(outs, tuple) else vmem,
        scratch_shapes=list(scratch),
        compiler_params=pltpu.CompilerParams(vmem_limit_bytes=limit),
        name=name,
    )(*arrays)


def swap(value, axis):
    return lax.ppermute(value, axis, [(0, 1), (1, 0)])


def body(activations, cotangents, statistics, owner):
    device = lax.axis_index(("x", "yl", "z4", "zp", "yh", "core")).astype(jnp.int32).reshape(1)
    array = jax.ShapeDtypeStruct
    own = statistics[0]
    tokens = activations.shape[0]

    other = call(
        theirs_kernel,
        "grad_theirs",
        array((BLOCKS, QUADS, HALF, LANES), bf16),
        (device, activations, cotangents),
        scratch=[
            pltpu.VMEM((2, tokens, HALF), bf16),
            pltpu.VMEM((COLS, tokens, BLOCK), bf16),
            pltpu.SemaphoreType.DMA((4,)),
        ],
        limit=GRAD_LIMIT,
    )
    packed = call(
        mine_kernel,
        "grad_mine",
        array((XS * QUADS, HALF + STATS, LANES), bf16),
        (device, activations, cotangents, swap(other, "core"), own),
    )
    reduced = call(
        reduce_kernel,
        "reduce",
        array((FAR, TILE + PAIR * STATS, LANES), bf16),
        (device, owner, exchange(packed, NEAR_AXES)),
    )
    gradient, stats = call(
        total_kernel,
        "total",
        (array((PARTS, TILE, LANES), bf16), array((PAIR, FAR, STATS, LANES), bf16)),
        (exchange(reduced, FAR_AXES),),
    )
    stats = jnp.concatenate([stats, swap(stats, "yl")])
    rows = call(
        unpack_kernel,
        "unpack",
        array((2, BLOCK, BLOCK), f32),
        (device, stats, swap(stats, "core")),
    )
    tiles = exchange(gradient, PLANE)
    pieces = call(
        root_kernel,
        "root",
        array((XS, OUT_ROWS + OWN_ROWS, BLOCK), f32),
        (device, owner, rows, tiles, swap(tiles, "core")),
        scratch=[
            pltpu.VMEM((BLOCK, BLOCK), bf16),
            pltpu.VMEM((2, BLOCK, BLOCK), f32),
            pltpu.VMEM((3, BLOCK, BLOCK), f32),
        ],
    )
    updated, direction = call(
        join_kernel,
        "join",
        (array((OWN_ROWS, BLOCK), f32), array((OUT_ROWS, COLS * BLOCK), f32)),
        (device, owner, own, exchange(pieces, "x")),
    )
    return updated[None], direction


def solution(mesh):
    sizes = {"x": 4, "yl": 2, "z4": 4, "zp": 2, "yh": 4, "core": 2}
    fine = Mesh(mesh.devices.reshape(tuple(sizes.values())), tuple(sizes))
    every = tuple(sizes)
    rep, shard = every[:2], every[2:]
    return jax.shard_map(
        body,
        mesh=fine,
        in_specs=(P(every, None), P(every, None), P(rep, shard, None), P()),
        out_specs=(P(rep, shard, None), P(shard, None)),
        check_vma=False,
    )
```

```python
import jax
import jax.numpy as jnp
from jax import lax
from jax.experimental import pallas as pl
from jax.experimental.pallas import tpu as pltpu
from jax.sharding import Mesh
from jax.sharding import PartitionSpec as P

ema_decay = 0.9
BLOCK = 512
HALF = BLOCK // 2
LANES = 128
BLOCKS = 4
ROOTS = 8
COLS = 2
XS = 4
PAIR = 2
CORES = 2
SHARDS = 64
QUADS = 4
FAR = 16
PARTS = QUADS * FAR
OUT_ROWS = 16
OWN_ROWS = 8
STATS = 32
TILE = 16
f32 = jnp.float32
bf16 = jnp.bfloat16
NEAR_AXES = ("x", "yl", "zp")
FAR_AXES = ("z4", "yh")
PLANE = ("yl", "zp") + FAR_AXES
VMEM_LIMIT = 40 * 1024 * 1024
GRAD_LIMIT = 60 * 1024 * 1024


def held_by(slot, owner_ref):
    held = jnp.int32(0)
    for root in range(1, ROOTS):
        held = jnp.where(owner_ref[root] == slot, root, held)
    return held


def near_place(device):
    return device // (PAIR * SHARDS), device // SHARDS % PAIR, device // 8 % PAIR, device % CORES


def theirs_kernel(device_ref, act_hbm, cot_hbm, out_hbm, act_ref, cot_ref, out_ref, sems, out_sems):
    half = 1 - device_ref[0] % CORES
    copies = []
    for row in range(2):
        start = pl.multiple_of(row * BLOCK + half * HALF, HALF)
        copies.append(
            pltpu.make_async_copy(act_hbm.at[:, pl.ds(start, HALF)], act_ref.at[row], sems.at[row])
        )
    for col in range(COLS):
        columns = pl.ds(col * BLOCK, BLOCK)
        copies.append(
            pltpu.make_async_copy(cot_hbm.at[:, columns], cot_ref.at[col], sems.at[2 + col])
        )
    for number in (0, 2, 3, 1):
        copies[number].start()
    sent = []
    for row in range(2):
        copies[row].wait()
        for col in range(COLS):
            if row == 0:
                copies[2 + col].wait()
            block = row * COLS + col
            term = half_term(act_ref[row], cot_ref[col]).astype(bf16)
            for lane in range(QUADS):
                out_ref[block, lane] = term[:, lane * LANES : (lane + 1) * LANES]
            sent.append(
                pltpu.make_async_copy(out_ref.at[block], out_hbm.at[block], out_sems.at[block])
            )
            sent[-1].start()
    for copy in sent:
        copy.wait()


def half_term(act, cot):
    return lax.dot_general(act, cot, (((0,), (0,)), ((), ())), preferred_element_type=f32)


def mine_kernel(device_ref, act_ref, cot_ref, other_ref, own_ref, out_ref):
    half = device_ref[0] % CORES
    parts = [own_ref[:, lane * LANES : (lane + 1) * LANES] for lane in range(BLOCK // LANES)]
    stats = jnp.concatenate(parts, axis=0).astype(bf16)
    for row in range(2):
        start = pl.multiple_of(row * BLOCK + half * HALF, HALF)
        act = act_ref[:, pl.ds(start, HALF)]
        for col in range(COLS):
            block = row * COLS + col
            term = half_term(act, cot_ref[:, col * BLOCK : (col + 1) * BLOCK])
            for lane in range(QUADS):
                total = term[:, lane * LANES : (lane + 1) * LANES] + other_ref[block, lane].astype(f32)
                out_ref[block * QUADS + lane, :HALF] = total.astype(bf16)
                out_ref[block * QUADS + lane, HALF:] = stats


def reduce_kernel(device_ref, owner_ref, terms_ref, out_ref):
    block = near_place(device_ref[0])[0]
    firsts = [owner_ref[side * BLOCKS + block] * PAIR for side in range(2)]
    stats = [terms_ref[first + low, HALF:] for first in firsts for low in range(PAIR)]
    for part in range(FAR):
        rows = slice(part * TILE, (part + 1) * TILE)
        total = terms_ref[0, rows].astype(f32)
        for source in range(1, XS * QUADS):
            total += terms_ref[source, rows].astype(f32)
        out_ref[part, :TILE] = total.astype(bf16)
        for quad in range(QUADS):
            out_ref[part, TILE + quad * STATS : TILE + (quad + 1) * STATS] = stats[quad]


def total_kernel(parts_ref, gradient_ref):
    total = parts_ref[0, :TILE].astype(f32)
    for part in range(1, FAR):
        total += parts_ref[part, :TILE].astype(f32)
    gradient = total.astype(bf16)
    for part in range(PARTS):
        gradient_ref[part] = gradient


def unpack_kernel(device_ref, parts_here_ref, parts_there_ref, stats):
    core = device_ref[0] % CORES
    for parts_ref, at in ((parts_here_ref, core), (parts_there_ref, 1 - core)):
        for quad in range(QUADS):
            side, low = divmod(quad, PAIR)
            for part in range(FAR):
                high, column = divmod(part, 4)
                value = parts_ref[part, TILE + quad * STATS : TILE + (quad + 1) * STATS].astype(f32)
                shard = (high * PAIR + low) * 8 + column * CORES + at
                place = pl.ds(pl.multiple_of(shard * OWN_ROWS, OWN_ROWS), OWN_ROWS)
                for lane in range(BLOCK // LANES):
                    columns = slice(lane * LANES, (lane + 1) * LANES)
                    stats[side, place, columns] = value[lane * OWN_ROWS : (lane + 1) * OWN_ROWS]


def product(left, right):
    return jnp.dot(left.astype(bf16), right.astype(bf16), preferred_element_type=f32)


def newton(stats, gram):
    sides = range(2)
    updated = [ema_decay * stats[side] + (1.0 - ema_decay) * gram[side] for side in sides]
    scales = [jnp.sqrt(jnp.sum(value * value, keepdims=True) + 1e-06) for value in updated]

    def step(state):
        low = [2.0 * state[side] - product(state[side], state[side]) for side in sides]
        high = [2.0 * low[side] - product(low[side], low[side]) for side in sides]
        return [1.25**4 * (state[side] - product(high[side], state[side])) for side in sides]

    first = [updated[side] * (0.2 / scales[side]) for side in sides]
    second = step(first)
    return first, second, step(second)


def root_rows(first, second, third, diagonal):
    own_first, own_second, own_third = first
    both = own_first + own_second - product(own_first, second)
    return 1.25**3 * (diagonal - (both + own_third - product(both, third)))


def root_kernel(
    device_ref,
    owner_ref,
    stats,
    tiles_here_ref,
    tiles_there_ref,
    out_ref,
    grad,
    gram,
    rows,
):
    device = device_ref[0]
    position = device % SHARDS
    _, near_y, _, core = near_place(device)
    for tiles_ref, at in ((tiles_here_ref, core), (tiles_there_ref, 1 - core)):
        for part in range(PARTS):
            lane, group = divmod(part, FAR)
            place = pl.ds(pl.multiple_of(at * HALF + group * TILE, TILE), TILE)
            grad[place, lane * LANES : (lane + 1) * LANES] = tiles_ref[part]
    gram[0] = lax.dot_general(
        grad[...], grad[...], (((1,), (1,)), ((), ())), preferred_element_type=f32
    )
    gram[1] = lax.dot_general(
        grad[...], grad[...], (((0,), (0,)), ((), ())), preferred_element_type=f32
    )
    own = pl.ds(pl.multiple_of(position * OWN_ROWS, OWN_ROWS), OWN_ROWS)
    for receiver in range(XS):
        held = held_by(receiver * PAIR + near_y, owner_ref)
        out_ref[receiver, OUT_ROWS:] = gram[held // BLOCKS, own, :]

    start = pl.multiple_of(position % (BLOCK // OUT_ROWS) * OUT_ROWS, OUT_ROWS)
    states = newton(stats, gram)
    left, right = [[state[side] for state in states] for side in range(2)]
    for number in range(3):
        rows[number] = left[number]
    own = tuple(rows[number, pl.ds(start, OUT_ROWS), :] for number in range(3))
    shape = (OUT_ROWS, BLOCK)
    diagonal = lax.broadcasted_iota(jnp.int32, shape, 0) + start == lax.broadcasted_iota(jnp.int32, shape, 1)
    left_rows = root_rows(own, left[1], left[2], jnp.where(diagonal, 1.0, 0.0)).astype(bf16)
    mixed = jnp.dot(left_rows, grad[...], preferred_element_type=f32).astype(bf16)

    shape = (BLOCK, BLOCK)
    diagonal = lax.broadcasted_iota(jnp.int32, shape, 0) == lax.broadcasted_iota(jnp.int32, shape, 1)
    right_root = root_rows(right, right[1], right[2], jnp.where(diagonal, 1.0, 0.0)).astype(bf16)
    piece = jnp.dot(mixed, right_root, preferred_element_type=f32)
    for receiver in range(XS):
        out_ref[receiver, :OUT_ROWS] = piece


def join_kernel(device_ref, owner_ref, own_ref, pieces_ref, updated_ref, direction_ref):
    device = device_ref[0]
    block = held_by(device // SHARDS, owner_ref) % BLOCKS
    updated_ref[...] = ema_decay * own_ref[...] + (1.0 - ema_decay) * pieces_ref[block, OUT_ROWS:]
    first = device % SHARDS // (BLOCK // OUT_ROWS) * COLS
    for col in range(COLS):
        direction_ref[:, col * BLOCK : (col + 1) * BLOCK] = pieces_ref[first + col, :OUT_ROWS]


def exchange(value, axes):
    return lax.all_to_all(value, axes, split_axis=0, concat_axis=0, tiled=True)


def call(kernel, name, outs, arrays, scratch=(), limit=VMEM_LIMIT):
    vmem = pl.BlockSpec(memory_space=pltpu.VMEM)
    smem = pl.BlockSpec(memory_space=pltpu.SMEM)
    rest = pl.BlockSpec(memory_space=pl.ANY) if limit > VMEM_LIMIT else vmem
    return pl.pallas_call(
        kernel,
        out_shape=outs,
        in_specs=[smem if array.ndim == 1 else rest for array in arrays],
        out_specs=tuple(rest for _ in outs) if isinstance(outs, tuple) else rest,
        scratch_shapes=list(scratch),
        compiler_params=pltpu.CompilerParams(vmem_limit_bytes=limit),
        name=name,
    )(*arrays)


def swap(value, axis):
    return lax.ppermute(value, axis, [(0, 1), (1, 0)])


def body(activations, cotangents, statistics, owner):
    device = lax.axis_index(("x", "yl", "z4", "zp", "yh", "core")).astype(jnp.int32).reshape(1)
    array = jax.ShapeDtypeStruct
    own = statistics[0]
    tokens = activations.shape[0]

    other = call(
        theirs_kernel,
        "grad_theirs",
        array((BLOCKS, QUADS, HALF, LANES), bf16),
        (device, activations, cotangents),
        scratch=[
            pltpu.VMEM((2, tokens, HALF), bf16),
            pltpu.VMEM((COLS, tokens, BLOCK), bf16),
            pltpu.VMEM((BLOCKS, QUADS, HALF, LANES), bf16),
            pltpu.SemaphoreType.DMA((4,)),
            pltpu.SemaphoreType.DMA((BLOCKS,)),
        ],
        limit=GRAD_LIMIT,
    )
    packed = call(
        mine_kernel,
        "grad_mine",
        array((XS * QUADS, HALF + STATS, LANES), bf16),
        (device, activations, cotangents, swap(other, "core"), own),
    )
    reduced = call(
        reduce_kernel,
        "reduce",
        array((FAR, TILE + QUADS * STATS, LANES), bf16),
        (device, owner, exchange(packed, NEAR_AXES)),
    )
    parts = exchange(reduced, FAR_AXES)
    gradient = call(total_kernel, "total", array((PARTS, TILE, LANES), bf16), (parts,))
    rows = call(
        unpack_kernel, "unpack", array((2, BLOCK, BLOCK), f32), (device, parts, swap(parts, "core"))
    )
    tiles = exchange(gradient, PLANE)
    pieces = call(
        root_kernel,
        "root",
        array((XS, OUT_ROWS + OWN_ROWS, BLOCK), f32),
        (device, owner, rows, tiles, swap(tiles, "core")),
        scratch=[
            pltpu.VMEM((BLOCK, BLOCK), bf16),
            pltpu.VMEM((2, BLOCK, BLOCK), f32),
            pltpu.VMEM((3, BLOCK, BLOCK), f32),
        ],
    )
    updated, direction = call(
        join_kernel,
        "join",
        (array((OWN_ROWS, BLOCK), f32), array((OUT_ROWS, COLS * BLOCK), f32)),
        (device, owner, own, exchange(pieces, "x")),
    )
    return updated[None], direction


def solution(mesh):
    sizes = {"x": 4, "yl": 2, "z4": 4, "zp": 2, "yh": 4, "core": 2}
    fine = Mesh(mesh.devices.reshape(tuple(sizes.values())), tuple(sizes))
    every = tuple(sizes)
    rep, shard = every[:2], every[2:]
    return jax.shard_map(
        body,
        mesh=fine,
        in_specs=(P(every, None), P(every, None), P(rep, shard, None), P()),
        out_specs=(P(rep, shard, None), P(shard, None)),
        check_vma=False,
    )
```

```python
import jax
import jax.numpy as jnp
from jax import lax
from jax.experimental import pallas as pl
from jax.experimental.pallas import tpu as pltpu
from jax.sharding import Mesh
from jax.sharding import PartitionSpec as P

ema_decay = 0.9
BLOCK = 512
HALF = BLOCK // 2
LANES = 128
BLOCKS = 4
ROOTS = 8
COLS = 2
XS = 4
PAIR = 2
CORES = 2
SHARDS = 64
QUADS = 4
FAR = 16
PARTS = QUADS * FAR
OUT_ROWS = 16
OWN_ROWS = 8
STATS = 32
GROUPS = 5
TILE = 16
f32 = jnp.float32
bf16 = jnp.bfloat16
NEAR_AXES = ("x", "yl", "zp")
FAR_AXES = ("z4", "yh")
PLANE = ("yl", "zp") + FAR_AXES
VMEM_LIMIT = 40 * 1024 * 1024
GRAD_LIMIT = 60 * 1024 * 1024


def held_by(slot, owner_ref):
    held = jnp.int32(0)
    for root in range(1, ROOTS):
        held = jnp.where(owner_ref[root] == slot, root, held)
    return held


def near_place(device):
    return device // (PAIR * SHARDS), device // SHARDS % PAIR, device // 8 % PAIR, device % CORES


def theirs_kernel(device_ref, act_hbm, cot_hbm, out_hbm, act_ref, cot_ref, out_ref, sems, out_sems):
    half = 1 - device_ref[0] % CORES
    copies = []
    for row in range(2):
        start = pl.multiple_of(row * BLOCK + half * HALF, HALF)
        copies.append(
            pltpu.make_async_copy(act_hbm.at[:, pl.ds(start, HALF)], act_ref.at[row], sems.at[row])
        )
    for col in range(COLS):
        columns = pl.ds(col * BLOCK, BLOCK)
        copies.append(
            pltpu.make_async_copy(cot_hbm.at[:, columns], cot_ref.at[col], sems.at[2 + col])
        )
    for number in (0, 2, 3, 1):
        copies[number].start()
    sent = []
    for row in range(2):
        copies[row].wait()
        for col in range(COLS):
            if row == 0:
                copies[2 + col].wait()
            block = row * COLS + col
            term = half_term(act_ref[row], cot_ref[col]).astype(bf16)
            for lane in range(QUADS):
                out_ref[block, lane] = term[:, lane * LANES : (lane + 1) * LANES]
            sent.append(
                pltpu.make_async_copy(out_ref.at[block], out_hbm.at[block], out_sems.at[block])
            )
            sent[-1].start()
    for copy in sent:
        copy.wait()


def half_term(act, cot):
    return lax.dot_general(act, cot, (((0,), (0,)), ((), ())), preferred_element_type=f32)


def mine_kernel(device_ref, act_ref, cot_ref, other_ref, own_ref, out_ref):
    half = device_ref[0] % CORES
    parts = [own_ref[:, lane * LANES : (lane + 1) * LANES] for lane in range(BLOCK // LANES)]
    stats = jnp.concatenate(parts, axis=0).astype(bf16)
    for row in range(2):
        start = pl.multiple_of(row * BLOCK + half * HALF, HALF)
        act = act_ref[:, pl.ds(start, HALF)]
        for col in range(COLS):
            block = row * COLS + col
            term = half_term(act, cot_ref[:, col * BLOCK : (col + 1) * BLOCK])
            for lane in range(QUADS):
                total = term[:, lane * LANES : (lane + 1) * LANES] + other_ref[block, lane].astype(f32)
                out_ref[block * QUADS + lane, :HALF] = total.astype(bf16)
                out_ref[block * QUADS + lane, HALF:] = stats


def sent_groups(row_block):
    near = [(side, (row_block + step) % 4) for side in range(2) for step in range(2)]
    return near + [(row_block // 2, (row_block + 2) % 4)]


def reduce_kernel(device_ref, owner_ref, terms_ref, out_ref):
    block = near_place(device_ref[0])[0]
    row_block = device_ref[0] % SHARDS // 16
    lanes = []
    for side in range(2):
        first = owner_ref[side * BLOCKS + block] * PAIR
        low, high = (terms_ref[first + chip, HALF:].astype(f32) for chip in range(PAIR))
        rows = [slice(lane * OWN_ROWS, (lane + 1) * OWN_ROWS) for lane in range(4)]
        lanes.append([jnp.concatenate([low[place], high[place]], axis=0) for place in rows])
    stats = []
    for group in range(GROUPS):
        chosen = None
        for number in range(4):
            side, lane = sent_groups(number)[group]
            here = lanes[side][lane]
            chosen = here if chosen is None else jnp.where(row_block == number, here, chosen)
        stats.append(chosen.astype(bf16))
    for part in range(FAR):
        rows = slice(part * TILE, (part + 1) * TILE)
        total = terms_ref[0, rows].astype(f32)
        for source in range(1, XS * QUADS):
            total += terms_ref[source, rows].astype(f32)
        out_ref[part, :TILE] = total.astype(bf16)
        for group in range(GROUPS):
            out_ref[part, TILE * (group + 1) : TILE * (group + 2)] = stats[group]


def total_kernel(parts_ref, gradient_ref):
    total = parts_ref[0, :TILE].astype(f32)
    for part in range(1, FAR):
        total += parts_ref[part, :TILE].astype(f32)
    gradient = total.astype(bf16)
    for part in range(PARTS):
        gradient_ref[part] = gradient


def unpack_kernel(device_ref, parts_here_ref, parts_there_ref, stats):
    core = device_ref[0] % CORES
    for parts_ref, at in ((parts_here_ref, core), (parts_there_ref, 1 - core)):
        for part in range(FAR):
            row_block, column = divmod(part, 4)
            for group, (side, lane) in enumerate(sent_groups(row_block)):
                value = parts_ref[part, TILE * (group + 1) : TILE * (group + 2)].astype(f32)
                for low in range(PAIR):
                    shard = (row_block * PAIR + low) * 8 + column * CORES + at
                    place = pl.ds(pl.multiple_of(shard * OWN_ROWS, OWN_ROWS), OWN_ROWS)
                    columns = slice(lane * LANES, (lane + 1) * LANES)
                    stats[side, place, columns] = value[low * OWN_ROWS : (low + 1) * OWN_ROWS]
    for row_block in range(4):
        for side, lane in sent_groups(row_block):
            if lane != row_block:
                rows = slice(row_block * LANES, (row_block + 1) * LANES)
                columns = slice(lane * LANES, (lane + 1) * LANES)
                stats[side, columns, rows] = stats[side, rows, columns].T


def product(left, right):
    return jnp.dot(left.astype(bf16), right.astype(bf16), preferred_element_type=f32)


def symmetric(left, right, dims=((1,), (0,))):
    left, right = left[...].astype(bf16), right[...].astype(bf16)
    (left_dim,), (right_dim,) = dims

    def part(rows, columns):
        first = left[rows] if left_dim == 1 else left[:, rows]
        second = right[:, columns] if right_dim == 0 else right[columns]
        return lax.dot_general(first, second, (dims, ((), ())), preferred_element_type=f32)

    low, high = slice(0, HALF), slice(HALF, BLOCK)
    top = part(low, slice(0, BLOCK))
    corner = part(high, high)
    return jnp.concatenate([top, jnp.concatenate([top[:, HALF:].T, corner], axis=1)], axis=0)


def newton(stats, gram):
    sides = range(2)
    updated = [ema_decay * stats[side] + (1.0 - ema_decay) * gram[side] for side in sides]
    scales = [jnp.sqrt(jnp.sum(value * value, keepdims=True) + 1e-06) for value in updated]

    def step(state):
        low = [2.0 * state[side] - symmetric(state[side], state[side]) for side in sides]
        high = [2.0 * low[side] - symmetric(low[side], low[side]) for side in sides]
        return [1.25**4 * (state[side] - symmetric(high[side], state[side])) for side in sides]

    first = [updated[side] * (0.2 / scales[side]) for side in sides]
    second = step(first)
    return first, second, step(second)


def root_rows(first, second, third, diagonal, times=product):
    own_first, own_second, own_third = first
    both = own_first + own_second - times(own_first, second)
    return 1.25**3 * (diagonal - (both + own_third - times(both, third)))


def root_kernel(
    device_ref,
    owner_ref,
    stats,
    tiles_here_ref,
    tiles_there_ref,
    out_ref,
    grad,
    gram,
    rows,
):
    device = device_ref[0]
    position = device % SHARDS
    _, near_y, _, core = near_place(device)
    for tiles_ref, at in ((tiles_here_ref, core), (tiles_there_ref, 1 - core)):
        for part in range(PARTS):
            lane, group = divmod(part, FAR)
            place = pl.ds(pl.multiple_of(at * HALF + group * TILE, TILE), TILE)
            grad[place, lane * LANES : (lane + 1) * LANES] = tiles_ref[part]
    gram[0] = symmetric(grad, grad, ((1,), (1,)))
    gram[1] = symmetric(grad, grad, ((0,), (0,)))
    own = pl.ds(pl.multiple_of(position * OWN_ROWS, OWN_ROWS), OWN_ROWS)
    for receiver in range(XS):
        held = held_by(receiver * PAIR + near_y, owner_ref)
        out_ref[receiver, OUT_ROWS:] = gram[held // BLOCKS, own, :]

    start = pl.multiple_of(position % (BLOCK // OUT_ROWS) * OUT_ROWS, OUT_ROWS)
    states = newton(stats, gram)
    left, right = [[state[side] for state in states] for side in range(2)]
    for number in range(3):
        rows[number] = left[number]
    own = tuple(rows[number, pl.ds(start, OUT_ROWS), :] for number in range(3))
    shape = (OUT_ROWS, BLOCK)
    diagonal = lax.broadcasted_iota(jnp.int32, shape, 0) + start == lax.broadcasted_iota(jnp.int32, shape, 1)
    left_rows = root_rows(own, left[1], left[2], jnp.where(diagonal, 1.0, 0.0)).astype(bf16)
    mixed = jnp.dot(left_rows, grad[...], preferred_element_type=f32).astype(bf16)

    shape = (BLOCK, BLOCK)
    diagonal = lax.broadcasted_iota(jnp.int32, shape, 0) == lax.broadcasted_iota(jnp.int32, shape, 1)
    right_root = root_rows(
        right, right[1], right[2], jnp.where(diagonal, 1.0, 0.0), symmetric
    ).astype(bf16)
    piece = jnp.dot(mixed, right_root, preferred_element_type=f32)
    for receiver in range(XS):
        out_ref[receiver, :OUT_ROWS] = piece


def join_kernel(device_ref, owner_ref, own_ref, pieces_ref, updated_ref, direction_ref):
    device = device_ref[0]
    block = held_by(device // SHARDS, owner_ref) % BLOCKS
    updated_ref[...] = ema_decay * own_ref[...] + (1.0 - ema_decay) * pieces_ref[block, OUT_ROWS:]
    first = device % SHARDS // (BLOCK // OUT_ROWS) * COLS
    for col in range(COLS):
        direction_ref[:, col * BLOCK : (col + 1) * BLOCK] = pieces_ref[first + col, :OUT_ROWS]


def exchange(value, axes):
    return lax.all_to_all(value, axes, split_axis=0, concat_axis=0, tiled=True)


def call(kernel, name, outs, arrays, scratch=(), limit=VMEM_LIMIT):
    vmem = pl.BlockSpec(memory_space=pltpu.VMEM)
    smem = pl.BlockSpec(memory_space=pltpu.SMEM)
    rest = pl.BlockSpec(memory_space=pl.ANY) if limit > VMEM_LIMIT else vmem
    return pl.pallas_call(
        kernel,
        out_shape=outs,
        in_specs=[smem if array.ndim == 1 else rest for array in arrays],
        out_specs=tuple(rest for _ in outs) if isinstance(outs, tuple) else rest,
        scratch_shapes=list(scratch),
        compiler_params=pltpu.CompilerParams(vmem_limit_bytes=limit),
        name=name,
    )(*arrays)


def swap(value, axis):
    return lax.ppermute(value, axis, [(0, 1), (1, 0)])


def body(activations, cotangents, statistics, owner):
    device = lax.axis_index(("x", "yl", "z4", "zp", "yh", "core")).astype(jnp.int32).reshape(1)
    array = jax.ShapeDtypeStruct
    own = statistics[0]
    tokens = activations.shape[0]

    other = call(
        theirs_kernel,
        "grad_theirs",
        array((BLOCKS, QUADS, HALF, LANES), bf16),
        (device, activations, cotangents),
        scratch=[
            pltpu.VMEM((2, tokens, HALF), bf16),
            pltpu.VMEM((COLS, tokens, BLOCK), bf16),
            pltpu.VMEM((BLOCKS, QUADS, HALF, LANES), bf16),
            pltpu.SemaphoreType.DMA((4,)),
            pltpu.SemaphoreType.DMA((BLOCKS,)),
        ],
        limit=GRAD_LIMIT,
    )
    packed = call(
        mine_kernel,
        "grad_mine",
        array((XS * QUADS, HALF + STATS, LANES), bf16),
        (device, activations, cotangents, swap(other, "core"), own),
    )
    reduced = call(
        reduce_kernel,
        "reduce",
        array((FAR, TILE * (1 + GROUPS), LANES), bf16),
        (device, owner, exchange(packed, NEAR_AXES)),
    )
    parts = exchange(reduced, FAR_AXES)
    gradient = call(total_kernel, "total", array((PARTS, TILE, LANES), bf16), (parts,))
    rows = call(
        unpack_kernel, "unpack", array((2, BLOCK, BLOCK), f32), (device, parts, swap(parts, "core"))
    )
    tiles = exchange(gradient, PLANE)
    pieces = call(
        root_kernel,
        "root",
        array((XS, OUT_ROWS + OWN_ROWS, BLOCK), f32),
        (device, owner, rows, tiles, swap(tiles, "core")),
        scratch=[
            pltpu.VMEM((BLOCK, BLOCK), bf16),
            pltpu.VMEM((2, BLOCK, BLOCK), f32),
            pltpu.VMEM((3, BLOCK, BLOCK), f32),
        ],
    )
    updated, direction = call(
        join_kernel,
        "join",
        (array((OWN_ROWS, BLOCK), f32), array((OUT_ROWS, COLS * BLOCK), f32)),
        (device, owner, own, exchange(pieces, "x")),
    )
    return updated[None], direction


def solution(mesh):
    sizes = {"x": 4, "yl": 2, "z4": 4, "zp": 2, "yh": 4, "core": 2}
    fine = Mesh(mesh.devices.reshape(tuple(sizes.values())), tuple(sizes))
    every = tuple(sizes)
    rep, shard = every[:2], every[2:]
    return jax.shard_map(
        body,
        mesh=fine,
        in_specs=(P(every, None), P(every, None), P(rep, shard, None), P()),
        out_specs=(P(rep, shard, None), P(shard, None)),
        check_vma=False,
    )
```

```python
import jax
import jax.numpy as jnp
from jax import lax
from jax.experimental import pallas as pl
from jax.experimental.pallas import tpu as pltpu
from jax.sharding import Mesh
from jax.sharding import PartitionSpec as P

ema_decay = 0.9
BLOCK = 512
HALF = BLOCK // 2
LANES = 128
BLOCKS = 4
ROOTS = 8
COLS = 2
XS = 4
PAIR = 2
CORES = 2
SHARDS = 64
QUADS = 4
FAR = 16
PARTS = QUADS * FAR
OUT_ROWS = 16
OWN_ROWS = 8
STATS = 32
GROUPS = 5
TILE = 16
f32 = jnp.float32
bf16 = jnp.bfloat16
NEAR_AXES = ("x", "yl", "zp")
FAR_AXES = ("z4", "yh")
PLANE = ("yl", "zp") + FAR_AXES
VMEM_LIMIT = 40 * 1024 * 1024
GRAD_LIMIT = 60 * 1024 * 1024


def held_by(slot, owner_ref):
    held = jnp.int32(0)
    for root in range(1, ROOTS):
        held = jnp.where(owner_ref[root] == slot, root, held)
    return held


def near_place(device):
    return device // (PAIR * SHARDS), device // SHARDS % PAIR, device // 8 % PAIR, device % CORES


def theirs_kernel(device_ref, act_hbm, cot_hbm, out_hbm, act_ref, cot_ref, out_ref, sems, out_sems):
    half = 1 - device_ref[0] % CORES
    copies = []
    for row in range(2):
        start = pl.multiple_of(row * BLOCK + half * HALF, HALF)
        copies.append(
            pltpu.make_async_copy(act_hbm.at[:, pl.ds(start, HALF)], act_ref.at[row], sems.at[row])
        )
    for col in range(COLS):
        columns = pl.ds(col * BLOCK, BLOCK)
        copies.append(
            pltpu.make_async_copy(cot_hbm.at[:, columns], cot_ref.at[col], sems.at[2 + col])
        )
    for number in (0, 2, 3, 1):
        copies[number].start()
    sent = []
    for row in range(2):
        copies[row].wait()
        for col in range(COLS):
            if row == 0:
                copies[2 + col].wait()
            block = row * COLS + col
            term = half_term(act_ref[row], cot_ref[col]).astype(bf16)
            for lane in range(QUADS):
                out_ref[block, lane] = term[:, lane * LANES : (lane + 1) * LANES]
            sent.append(
                pltpu.make_async_copy(out_ref.at[block], out_hbm.at[block], out_sems.at[block])
            )
            sent[-1].start()
    for copy in sent:
        copy.wait()


def half_term(act, cot):
    return lax.dot_general(act, cot, (((0,), (0,)), ((), ())), preferred_element_type=f32)


def mine_kernel(device_ref, act_ref, cot_ref, other_ref, own_ref, out_ref):
    half = device_ref[0] % CORES
    parts = [own_ref[:, lane * LANES : (lane + 1) * LANES] for lane in range(BLOCK // LANES)]
    stats = jnp.concatenate(parts, axis=0).astype(bf16)
    for row in range(2):
        start = pl.multiple_of(row * BLOCK + half * HALF, HALF)
        act = act_ref[:, pl.ds(start, HALF)]
        for col in range(COLS):
            block = row * COLS + col
            term = half_term(act, cot_ref[:, col * BLOCK : (col + 1) * BLOCK])
            for lane in range(QUADS):
                total = term[:, lane * LANES : (lane + 1) * LANES] + other_ref[block, lane].astype(f32)
                out_ref[block * QUADS + lane, :HALF] = total.astype(bf16)
                out_ref[block * QUADS + lane, HALF:] = stats


def slots_kernel(device_ref, owner_ref, out_ref):
    block = near_place(device_ref[0])[0]
    for side in range(2):
        out_ref[side] = owner_ref[side * BLOCKS + block] * PAIR


def sent_groups(row_block):
    near = [(side, (row_block + step) % 4) for side in range(2) for step in range(2)]
    return near + [(row_block // 2, (row_block + 2) % 4)]


def reduce_kernel(device_ref, slots_ref, terms_ref, out_ref):
    row_block = device_ref[0] % SHARDS // 16
    lanes = []
    for side in range(2):
        first = slots_ref[side]
        low, high = (terms_ref[first + chip, HALF:].astype(f32) for chip in range(PAIR))
        rows = [slice(lane * OWN_ROWS, (lane + 1) * OWN_ROWS) for lane in range(4)]
        lanes.append([jnp.concatenate([low[place], high[place]], axis=0) for place in rows])
    stats = []
    for group in range(GROUPS):
        chosen = None
        for number in range(4):
            side, lane = sent_groups(number)[group]
            here = lanes[side][lane]
            chosen = here if chosen is None else jnp.where(row_block == number, here, chosen)
        stats.append(chosen.astype(bf16))
    for part in range(FAR):
        rows = slice(part * TILE, (part + 1) * TILE)
        total = terms_ref[0, rows].astype(f32)
        for source in range(1, XS * QUADS):
            total += terms_ref[source, rows].astype(f32)
        out_ref[part, :TILE] = total.astype(bf16)
        for group in range(GROUPS):
            out_ref[part, TILE * (group + 1) : TILE * (group + 2)] = stats[group]


def total_kernel(parts_ref, gradient_ref):
    total = parts_ref[0, :TILE].astype(f32)
    for part in range(1, FAR):
        total += parts_ref[part, :TILE].astype(f32)
    gradient = total.astype(bf16)
    for part in range(PARTS):
        gradient_ref[part] = gradient


def unpack_kernel(device_ref, parts_here_ref, parts_there_ref, stats):
    core = device_ref[0] % CORES
    for parts_ref, at in ((parts_here_ref, core), (parts_there_ref, 1 - core)):
        for part in range(FAR):
            row_block, column = divmod(part, 4)
            for group, (side, lane) in enumerate(sent_groups(row_block)):
                value = parts_ref[part, TILE * (group + 1) : TILE * (group + 2)].astype(f32)
                for low in range(PAIR):
                    shard = (row_block * PAIR + low) * 8 + column * CORES + at
                    place = pl.ds(pl.multiple_of(shard * OWN_ROWS, OWN_ROWS), OWN_ROWS)
                    columns = slice(lane * LANES, (lane + 1) * LANES)
                    stats[side, place, columns] = value[low * OWN_ROWS : (low + 1) * OWN_ROWS]
    for row_block in range(4):
        for side, lane in sent_groups(row_block):
            if lane != row_block:
                rows = slice(row_block * LANES, (row_block + 1) * LANES)
                columns = slice(lane * LANES, (lane + 1) * LANES)
                stats[side, columns, rows] = stats[side, rows, columns].T


def product(left, right):
    return jnp.dot(left.astype(bf16), right.astype(bf16), preferred_element_type=f32)


def symmetric(left, right, dims=((1,), (0,))):
    left, right = left[...].astype(bf16), right[...].astype(bf16)
    (left_dim,), (right_dim,) = dims

    def part(rows, columns):
        first = left[rows] if left_dim == 1 else left[:, rows]
        second = right[:, columns] if right_dim == 0 else right[columns]
        return lax.dot_general(first, second, (dims, ((), ())), preferred_element_type=f32)

    low, high = slice(0, HALF), slice(HALF, BLOCK)
    top = part(low, slice(0, BLOCK))
    corner = part(high, high)
    return jnp.concatenate([top, jnp.concatenate([top[:, HALF:].T, corner], axis=1)], axis=0)


def newton(stats, gram):
    sides = range(2)
    updated = [ema_decay * stats[side] + (1.0 - ema_decay) * gram[side] for side in sides]
    scales = [jnp.sqrt(jnp.sum(value * value, keepdims=True) + 1e-06) for value in updated]

    def step(state):
        low = [2.0 * state[side] - symmetric(state[side], state[side]) for side in sides]
        high = [2.0 * low[side] - symmetric(low[side], low[side]) for side in sides]
        return [1.25**4 * (state[side] - symmetric(high[side], state[side])) for side in sides]

    first = [updated[side] * (0.2 / scales[side]) for side in sides]
    second = step(first)
    return first, second, step(second)


def root_rows(first, second, third, diagonal, times=product):
    own_first, own_second, own_third = first
    both = own_first + own_second - times(own_first, second)
    return 1.25**3 * (diagonal - (both + own_third - times(both, third)))


def root_kernel(
    device_ref,
    owner_ref,
    stats,
    tiles_here_ref,
    tiles_there_ref,
    out_ref,
    grad,
    gram,
    rows,
):
    device = device_ref[0]
    position = device % SHARDS
    _, near_y, _, core = near_place(device)
    for tiles_ref, at in ((tiles_here_ref, core), (tiles_there_ref, 1 - core)):
        for part in range(PARTS):
            lane, group = divmod(part, FAR)
            place = pl.ds(pl.multiple_of(at * HALF + group * TILE, TILE), TILE)
            grad[place, lane * LANES : (lane + 1) * LANES] = tiles_ref[part]
    gram[0] = symmetric(grad, grad, ((1,), (1,)))
    gram[1] = symmetric(grad, grad, ((0,), (0,)))
    own = pl.ds(pl.multiple_of(position * OWN_ROWS, OWN_ROWS), OWN_ROWS)
    for receiver in range(XS):
        held = held_by(receiver * PAIR + near_y, owner_ref)
        out_ref[receiver, OUT_ROWS:] = gram[held // BLOCKS, own, :]

    start = pl.multiple_of(position % (BLOCK // OUT_ROWS) * OUT_ROWS, OUT_ROWS)
    states = newton(stats, gram)
    left, right = [[state[side] for state in states] for side in range(2)]
    for number in range(3):
        rows[number] = left[number]
    own = tuple(rows[number, pl.ds(start, OUT_ROWS), :] for number in range(3))
    shape = (OUT_ROWS, BLOCK)
    diagonal = lax.broadcasted_iota(jnp.int32, shape, 0) + start == lax.broadcasted_iota(jnp.int32, shape, 1)
    left_rows = root_rows(own, left[1], left[2], jnp.where(diagonal, 1.0, 0.0)).astype(bf16)
    mixed = jnp.dot(left_rows, grad[...], preferred_element_type=f32).astype(bf16)

    shape = (BLOCK, BLOCK)
    diagonal = lax.broadcasted_iota(jnp.int32, shape, 0) == lax.broadcasted_iota(jnp.int32, shape, 1)
    right_root = root_rows(
        right, right[1], right[2], jnp.where(diagonal, 1.0, 0.0), symmetric
    ).astype(bf16)
    piece = jnp.dot(mixed, right_root, preferred_element_type=f32)
    for receiver in range(XS):
        out_ref[receiver, :OUT_ROWS] = piece


def join_kernel(device_ref, owner_ref, own_ref, pieces_ref, updated_ref, direction_ref):
    device = device_ref[0]
    block = held_by(device // SHARDS, owner_ref) % BLOCKS
    updated_ref[...] = ema_decay * own_ref[...] + (1.0 - ema_decay) * pieces_ref[block, OUT_ROWS:]
    first = device % SHARDS // (BLOCK // OUT_ROWS) * COLS
    for col in range(COLS):
        direction_ref[:, col * BLOCK : (col + 1) * BLOCK] = pieces_ref[first + col, :OUT_ROWS]


def exchange(value, axes):
    return lax.all_to_all(value, axes, split_axis=0, concat_axis=0, tiled=True)


vmem = pl.BlockSpec(memory_space=pltpu.VMEM)
smem = pl.BlockSpec(memory_space=pltpu.SMEM)
anywhere = pl.BlockSpec(memory_space=pl.ANY)


def call(kernel, name, outs, arrays, scratch=(), limit=VMEM_LIMIT, operands=vmem, results=vmem):
    return pl.pallas_call(
        kernel,
        out_shape=outs,
        in_specs=[smem if array.ndim == 1 else operands for array in arrays],
        out_specs=tuple(results for _ in outs) if isinstance(outs, tuple) else results,
        scratch_shapes=list(scratch),
        compiler_params=pltpu.CompilerParams(vmem_limit_bytes=limit),
        name=name,
    )(*arrays)


def swap(value, axis):
    return lax.ppermute(value, axis, [(0, 1), (1, 0)])


def body(activations, cotangents, statistics, owner):
    device = lax.axis_index(("x", "yl", "z4", "zp", "yh", "core")).astype(jnp.int32).reshape(1)
    array = jax.ShapeDtypeStruct
    own = statistics[0]
    tokens = activations.shape[0]

    other = call(
        theirs_kernel,
        "grad_theirs",
        array((BLOCKS, QUADS, HALF, LANES), bf16),
        (device, activations, cotangents),
        scratch=[
            pltpu.VMEM((2, tokens, HALF), bf16),
            pltpu.VMEM((COLS, tokens, BLOCK), bf16),
            pltpu.VMEM((BLOCKS, QUADS, HALF, LANES), bf16),
            pltpu.SemaphoreType.DMA((4,)),
            pltpu.SemaphoreType.DMA((BLOCKS,)),
        ],
        limit=GRAD_LIMIT,
        operands=anywhere,
        results=anywhere,
    )
    packed = call(
        mine_kernel,
        "grad_mine",
        array((XS * QUADS, HALF + STATS, LANES), bf16),
        (device, activations, cotangents, swap(other, "core"), own),
    )
    slots = call(
        slots_kernel, "slots", array((2,), jnp.int32), (device, owner), results=smem
    )
    reduced = call(
        reduce_kernel,
        "reduce",
        array((FAR, TILE * (1 + GROUPS), LANES), bf16),
        (device, slots, exchange(packed, NEAR_AXES)),
    )
    parts = exchange(reduced, FAR_AXES)
    gradient = call(total_kernel, "total", array((PARTS, TILE, LANES), bf16), (parts,))
    rows = call(
        unpack_kernel, "unpack", array((2, BLOCK, BLOCK), f32), (device, parts, swap(parts, "core"))
    )
    tiles = exchange(gradient, PLANE)
    pieces = call(
        root_kernel,
        "root",
        array((XS, OUT_ROWS + OWN_ROWS, BLOCK), f32),
        (device, owner, rows, tiles, swap(tiles, "core")),
        scratch=[
            pltpu.VMEM((BLOCK, BLOCK), bf16),
            pltpu.VMEM((2, BLOCK, BLOCK), f32),
            pltpu.VMEM((3, BLOCK, BLOCK), f32),
        ],
    )
    updated, direction = call(
        join_kernel,
        "join",
        (array((OWN_ROWS, BLOCK), f32), array((OUT_ROWS, COLS * BLOCK), f32)),
        (device, owner, own, exchange(pieces, "x")),
    )
    return updated[None], direction


def solution(mesh):
    sizes = {"x": 4, "yl": 2, "z4": 4, "zp": 2, "yh": 4, "core": 2}
    fine = Mesh(mesh.devices.reshape(tuple(sizes.values())), tuple(sizes))
    every = tuple(sizes)
    rep, shard = every[:2], every[2:]
    return jax.shard_map(
        body,
        mesh=fine,
        in_specs=(P(every, None), P(every, None), P(rep, shard, None), P()),
        out_specs=(P(rep, shard, None), P(shard, None)),
        check_vma=False,
    )
```

```python
import jax
import jax.numpy as jnp
from jax import lax
from jax.experimental import pallas as pl
from jax.experimental.pallas import tpu as pltpu
from jax.sharding import Mesh
from jax.sharding import PartitionSpec as P

ema_decay = 0.9
BLOCK = 512
HALF = BLOCK // 2
LANES = 128
BLOCKS = 4
ROOTS = 8
COLS = 2
XS = 4
PAIR = 2
CORES = 2
SHARDS = 64
QUADS = 4
FAR = 16
PARTS = QUADS * FAR
OUT_ROWS = 16
OWN_ROWS = 8
STATS = 32
GROUPS = 5
TILE = 16
f32 = jnp.float32
bf16 = jnp.bfloat16
NEAR_AXES = ("x", "yl", "zp")
FAR_AXES = ("z4", "yh")
PLANE = ("yl", "zp") + FAR_AXES
DEVICE_AXES = ("x", "yl", "z4", "zp", "yh", "core")
VMEM_LIMIT = 40 * 1024 * 1024
GRAD_LIMIT = 60 * 1024 * 1024


def held_by(slot, owner_ref):
    held = jnp.int32(0)
    for root in range(1, ROOTS):
        held = jnp.where(owner_ref[root] == slot, root, held)
    return held


def this_device():
    return lax.axis_index(DEVICE_AXES)


def near_place(device):
    return device // (PAIR * SHARDS), device // SHARDS % PAIR, device // 8 % PAIR, device % CORES


def theirs_kernel(act_hbm, cot_hbm, out_hbm, act_ref, cot_ref, out_ref, sems, out_sems):
    half = 1 - this_device() % CORES
    copies = []
    for row in range(2):
        start = pl.multiple_of(row * BLOCK + half * HALF, HALF)
        copies.append(
            pltpu.make_async_copy(act_hbm.at[:, pl.ds(start, HALF)], act_ref.at[row], sems.at[row])
        )
    for col in range(COLS):
        columns = pl.ds(col * BLOCK, BLOCK)
        copies.append(
            pltpu.make_async_copy(cot_hbm.at[:, columns], cot_ref.at[col], sems.at[2 + col])
        )
    for number in (0, 2, 3, 1):
        copies[number].start()
    sent = []
    for row in range(2):
        copies[row].wait()
        for col in range(COLS):
            if row == 0:
                copies[2 + col].wait()
            block = row * COLS + col
            term = half_term(act_ref[row], cot_ref[col]).astype(bf16)
            for lane in range(QUADS):
                out_ref[block, lane] = term[:, lane * LANES : (lane + 1) * LANES]
            sent.append(
                pltpu.make_async_copy(out_ref.at[block], out_hbm.at[block], out_sems.at[block])
            )
            sent[-1].start()
    for copy in sent:
        copy.wait()


def half_term(act, cot):
    return lax.dot_general(act, cot, (((0,), (0,)), ((), ())), preferred_element_type=f32)


def mine_kernel(act_ref, cot_ref, out_ref):
    half = this_device() % CORES
    for row in range(2):
        start = pl.multiple_of(row * BLOCK + half * HALF, HALF)
        act = act_ref[:, pl.ds(start, HALF)]
        for col in range(COLS):
            term = half_term(act, cot_ref[:, col * BLOCK : (col + 1) * BLOCK])
            for lane in range(QUADS):
                out_ref[row * COLS + col, lane] = term[:, lane * LANES : (lane + 1) * LANES]


def pack_kernel(mine_ref, other_ref, own_ref, out_ref):
    parts = [own_ref[:, lane * LANES : (lane + 1) * LANES] for lane in range(BLOCK // LANES)]
    stats = jnp.concatenate(parts, axis=0).astype(bf16)
    for block in range(BLOCKS):
        for lane in range(QUADS):
            total = mine_ref[block, lane] + other_ref[block, lane].astype(f32)
            out_ref[block * QUADS + lane, :HALF] = total.astype(bf16)
            out_ref[block * QUADS + lane, HALF:] = stats


def sent_groups(row_block):
    near = [(side, (row_block + step) % 4) for side in range(2) for step in range(2)]
    return near + [(row_block // 2, (row_block + 2) % 4)]


def reduce_kernel(owner_ref, terms_ref, out_ref):
    block = near_place(this_device())[0]
    row_block = this_device() % SHARDS // 16
    lanes = []
    for side in range(2):
        first = owner_ref[side * BLOCKS + block] * PAIR
        low, high = (terms_ref[first + chip, HALF:].astype(f32) for chip in range(PAIR))
        rows = [slice(lane * OWN_ROWS, (lane + 1) * OWN_ROWS) for lane in range(4)]
        lanes.append([jnp.concatenate([low[place], high[place]], axis=0) for place in rows])
    stats = []
    for group in range(GROUPS):
        chosen = None
        for number in range(4):
            side, lane = sent_groups(number)[group]
            here = lanes[side][lane]
            chosen = here if chosen is None else jnp.where(row_block == number, here, chosen)
        stats.append(chosen.astype(bf16))
    for part in range(FAR):
        rows = slice(part * TILE, (part + 1) * TILE)
        total = terms_ref[0, rows].astype(f32)
        for source in range(1, XS * QUADS):
            total += terms_ref[source, rows].astype(f32)
        out_ref[part, :TILE] = total.astype(bf16)
        for group in range(GROUPS):
            out_ref[part, TILE * (group + 1) : TILE * (group + 2)] = stats[group]


def total_kernel(parts_ref, gradient_ref):
    total = parts_ref[0, :TILE].astype(f32)
    for part in range(1, FAR):
        total += parts_ref[part, :TILE].astype(f32)
    gradient = total.astype(bf16)
    for part in range(PARTS):
        gradient_ref[part] = gradient


def unpack_kernel(parts_here_ref, parts_there_ref, stats):
    core = this_device() % CORES
    for parts_ref, at in ((parts_here_ref, core), (parts_there_ref, 1 - core)):
        for part in range(FAR):
            row_block, column = divmod(part, 4)
            for group, (side, lane) in enumerate(sent_groups(row_block)):
                value = parts_ref[part, TILE * (group + 1) : TILE * (group + 2)].astype(f32)
                for low in range(PAIR):
                    shard = (row_block * PAIR + low) * 8 + column * CORES + at
                    place = pl.ds(pl.multiple_of(shard * OWN_ROWS, OWN_ROWS), OWN_ROWS)
                    columns = slice(lane * LANES, (lane + 1) * LANES)
                    stats[side, place, columns] = value[low * OWN_ROWS : (low + 1) * OWN_ROWS]
    for row_block in range(4):
        for side, lane in sent_groups(row_block):
            if lane != row_block:
                rows = slice(row_block * LANES, (row_block + 1) * LANES)
                columns = slice(lane * LANES, (lane + 1) * LANES)
                stats[side, columns, rows] = stats[side, rows, columns].T


def product(left, right):
    return jnp.dot(left.astype(bf16), right.astype(bf16), preferred_element_type=f32)


def symmetric(left, right, dims=((1,), (0,))):
    left, right = left[...].astype(bf16), right[...].astype(bf16)
    (left_dim,), (right_dim,) = dims

    def part(rows, columns):
        first = left[rows] if left_dim == 1 else left[:, rows]
        second = right[:, columns] if right_dim == 0 else right[columns]
        return lax.dot_general(first, second, (dims, ((), ())), preferred_element_type=f32)

    low, high = slice(0, HALF), slice(HALF, BLOCK)
    top = part(low, slice(0, BLOCK))
    corner = part(high, high)
    return jnp.concatenate([top, jnp.concatenate([top[:, HALF:].T, corner], axis=1)], axis=0)


def newton(stats, gram):
    sides = range(2)
    updated = [ema_decay * stats[side] + (1.0 - ema_decay) * gram[side] for side in sides]
    scales = [jnp.sqrt(jnp.sum(value * value, keepdims=True) + 1e-06) for value in updated]

    def step(state):
        low = [2.0 * state[side] - symmetric(state[side], state[side]) for side in sides]
        high = [2.0 * low[side] - symmetric(low[side], low[side]) for side in sides]
        return [1.25**4 * (state[side] - symmetric(high[side], state[side])) for side in sides]

    first = [updated[side] * (0.2 / scales[side]) for side in sides]
    second = step(first)
    return first, second, step(second)


def root_rows(first, second, third, diagonal, times=product):
    own_first, own_second, own_third = first
    both = own_first + own_second - times(own_first, second)
    return 1.25**3 * (diagonal - (both + own_third - times(both, third)))


def root_kernel(
    owner_ref,
    stats,
    tiles_here_ref,
    tiles_there_ref,
    out_ref,
    grad,
    gram,
    rows,
):
    device = this_device()
    position = device % SHARDS
    block, near_y, _, core = near_place(device)
    for tiles_ref, at in ((tiles_here_ref, core), (tiles_there_ref, 1 - core)):
        for part in range(PARTS):
            lane, group = divmod(part, FAR)
            place = pl.ds(pl.multiple_of(at * HALF + group * TILE, TILE), TILE)
            grad[place, lane * LANES : (lane + 1) * LANES] = tiles_ref[part]
    gram[0] = symmetric(grad, grad, ((1,), (1,)))
    gram[1] = symmetric(grad, grad, ((0,), (0,)))
    own = pl.ds(pl.multiple_of(position * OWN_ROWS, OWN_ROWS), OWN_ROWS)
    for receiver in range(XS):
        held = held_by(receiver * PAIR + near_y, owner_ref)
        here = held % BLOCKS == block
        out_ref[receiver, OUT_ROWS:] = jnp.where(here, gram[held // BLOCKS, own, :], 0.0)

    start = pl.multiple_of(position % (BLOCK // OUT_ROWS) * OUT_ROWS, OUT_ROWS)
    states = newton(stats, gram)
    left, right = [[state[side] for state in states] for side in range(2)]
    for number in range(3):
        rows[number] = left[number]
    own = tuple(rows[number, pl.ds(start, OUT_ROWS), :] for number in range(3))
    shape = (OUT_ROWS, BLOCK)
    diagonal = lax.broadcasted_iota(jnp.int32, shape, 0) + start == lax.broadcasted_iota(jnp.int32, shape, 1)
    left_rows = root_rows(own, left[1], left[2], jnp.where(diagonal, 1.0, 0.0)).astype(bf16)
    mixed = jnp.dot(left_rows, grad[...], preferred_element_type=f32).astype(bf16)

    shape = (BLOCK, BLOCK)
    diagonal = lax.broadcasted_iota(jnp.int32, shape, 0) == lax.broadcasted_iota(jnp.int32, shape, 1)
    right_root = root_rows(
        right, right[1], right[2], jnp.where(diagonal, 1.0, 0.0), symmetric
    ).astype(bf16)
    piece = jnp.dot(mixed, right_root, preferred_element_type=f32)
    for receiver in range(XS):
        out_ref[receiver, :OUT_ROWS] = piece


def join_kernel(own_ref, pieces_ref, updated_ref, direction_ref):
    rows = pieces_ref[0, OUT_ROWS:]
    for source in range(1, XS):
        rows += pieces_ref[source, OUT_ROWS:]
    updated_ref[...] = ema_decay * own_ref[...] + (1.0 - ema_decay) * rows
    first = this_device() % SHARDS // (BLOCK // OUT_ROWS) * COLS
    for col in range(COLS):
        direction_ref[:, col * BLOCK : (col + 1) * BLOCK] = pieces_ref[first + col, :OUT_ROWS]


def exchange(value, axes):
    return lax.all_to_all(value, axes, split_axis=0, concat_axis=0, tiled=True)


def call(kernel, name, outs, arrays, scratch=(), limit=VMEM_LIMIT):
    vmem = pl.BlockSpec(memory_space=pltpu.VMEM)
    smem = pl.BlockSpec(memory_space=pltpu.SMEM)
    rest = pl.BlockSpec(memory_space=pl.ANY) if limit > VMEM_LIMIT else vmem
    return pl.pallas_call(
        kernel,
        out_shape=outs,
        in_specs=[smem if array.ndim == 1 else rest for array in arrays],
        out_specs=tuple(rest for _ in outs) if isinstance(outs, tuple) else rest,
        scratch_shapes=list(scratch),
        compiler_params=pltpu.CompilerParams(vmem_limit_bytes=limit),
        name=name,
    )(*arrays)


def swap(value, axis):
    return lax.ppermute(value, axis, [(0, 1), (1, 0)])


def body(activations, cotangents, statistics, owner):
    array = jax.ShapeDtypeStruct
    own = statistics[0]
    tokens = activations.shape[0]

    other = call(
        theirs_kernel,
        "grad_theirs",
        array((BLOCKS, QUADS, HALF, LANES), bf16),
        (activations, cotangents),
        scratch=[
            pltpu.VMEM((2, tokens, HALF), bf16),
            pltpu.VMEM((COLS, tokens, BLOCK), bf16),
            pltpu.VMEM((BLOCKS, QUADS, HALF, LANES), bf16),
            pltpu.SemaphoreType.DMA((4,)),
            pltpu.SemaphoreType.DMA((BLOCKS,)),
        ],
        limit=GRAD_LIMIT,
    )
    mine = call(
        mine_kernel,
        "grad_mine",
        array((BLOCKS, QUADS, HALF, LANES), f32),
        (activations, cotangents),
    )
    packed = call(
        pack_kernel,
        "pack",
        array((XS * QUADS, HALF + STATS, LANES), bf16),
        (mine, swap(other, "core"), own),
    )
    reduced = call(
        reduce_kernel,
        "reduce",
        array((FAR, TILE * (1 + GROUPS), LANES), bf16),
        (owner, exchange(packed, NEAR_AXES)),
    )
    parts = exchange(reduced, FAR_AXES)
    gradient = call(total_kernel, "total", array((PARTS, TILE, LANES), bf16), (parts,))
    rows = call(
        unpack_kernel, "unpack", array((2, BLOCK, BLOCK), f32), (parts, swap(parts, "core"))
    )
    tiles = exchange(gradient, PLANE)
    pieces = call(
        root_kernel,
        "root",
        array((XS, OUT_ROWS + OWN_ROWS, BLOCK), f32),
        (owner, rows, tiles, swap(tiles, "core")),
        scratch=[
            pltpu.VMEM((BLOCK, BLOCK), bf16),
            pltpu.VMEM((2, BLOCK, BLOCK), f32),
            pltpu.VMEM((3, BLOCK, BLOCK), f32),
        ],
    )
    updated, direction = call(
        join_kernel,
        "join",
        (array((OWN_ROWS, BLOCK), f32), array((OUT_ROWS, COLS * BLOCK), f32)),
        (own, exchange(pieces, "x")),
    )
    return updated[None], direction


def solution(mesh):
    sizes = {"x": 4, "yl": 2, "z4": 4, "zp": 2, "yh": 4, "core": 2}
    fine = Mesh(mesh.devices.reshape(tuple(sizes.values())), tuple(sizes))
    every = tuple(sizes)
    rep, shard = every[:2], every[2:]
    return jax.shard_map(
        body,
        mesh=fine,
        in_specs=(P(every, None), P(every, None), P(rep, shard, None), P()),
        out_specs=(P(rep, shard, None), P(shard, None)),
        check_vma=False,
    )
```

```python
import jax
import jax.numpy as jnp
from jax import lax
from jax.experimental import pallas as pl
from jax.experimental.pallas import tpu as pltpu
from jax.sharding import Mesh
from jax.sharding import PartitionSpec as P

ema_decay = 0.9
BLOCK = 512
HALF = BLOCK // 2
LANES = 128
BLOCKS = 4
ROOTS = 8
COLS = 2
XS = 4
PAIR = 2
CORES = 2
SHARDS = 64
QUADS = 4
FAR = 16
PARTS = QUADS * FAR
OUT_ROWS = 16
OWN_ROWS = 8
STATS = 32
GROUPS = 5
TILE = 16
f32 = jnp.float32
bf16 = jnp.bfloat16
NEAR_AXES = ("x", "yl", "zp")
FAR_AXES = ("z4", "yh")
PLANE = ("yl", "zp") + FAR_AXES
DEVICE_AXES = ("x", "yl", "z4", "zp", "yh", "core")
VMEM_LIMIT = 40 * 1024 * 1024
GRAD_LIMIT = 60 * 1024 * 1024


def held_by(slot, owners_ref):
    held = jnp.zeros((1, LANES), jnp.int32)
    for root in range(1, ROOTS):
        held = jnp.where(owners_ref[root : root + 1] == slot, root, held)
    return held


def this_device():
    return lax.axis_index(DEVICE_AXES)


def near_place(device):
    return device // (PAIR * SHARDS), device // SHARDS % PAIR, device // 8 % PAIR, device % CORES


def theirs_kernel(act_hbm, cot_hbm, out_hbm, act_ref, cot_ref, out_ref, sems, out_sems):
    half = 1 - this_device() % CORES
    copies = []
    for row in range(2):
        start = pl.multiple_of(row * BLOCK + half * HALF, HALF)
        copies.append(
            pltpu.make_async_copy(act_hbm.at[:, pl.ds(start, HALF)], act_ref.at[row], sems.at[row])
        )
    for col in range(COLS):
        columns = pl.ds(col * BLOCK, BLOCK)
        copies.append(
            pltpu.make_async_copy(cot_hbm.at[:, columns], cot_ref.at[col], sems.at[2 + col])
        )
    for number in (0, 2, 3, 1):
        copies[number].start()
    sent = []
    for row in range(2):
        copies[row].wait()
        for col in range(COLS):
            if row == 0:
                copies[2 + col].wait()
            block = row * COLS + col
            term = half_term(act_ref[row], cot_ref[col]).astype(bf16)
            for lane in range(QUADS):
                out_ref[block, lane] = term[:, lane * LANES : (lane + 1) * LANES]
            sent.append(
                pltpu.make_async_copy(out_ref.at[block], out_hbm.at[block], out_sems.at[block])
            )
            sent[-1].start()
    for copy in sent:
        copy.wait()


def half_term(act, cot):
    return lax.dot_general(act, cot, (((0,), (0,)), ((), ())), preferred_element_type=f32)


def mine_kernel(owner_ref, act_ref, cot_ref, out_ref, owners_ref):
    for root in range(ROOTS):
        owners_ref[root : root + 1] = jnp.full((1, LANES), owner_ref[root], jnp.int32)
    half = this_device() % CORES
    for row in range(2):
        start = pl.multiple_of(row * BLOCK + half * HALF, HALF)
        act = act_ref[:, pl.ds(start, HALF)]
        for col in range(COLS):
            term = half_term(act, cot_ref[:, col * BLOCK : (col + 1) * BLOCK])
            for lane in range(QUADS):
                out_ref[row * COLS + col, lane] = term[:, lane * LANES : (lane + 1) * LANES]


def pack_kernel(mine_ref, other_ref, own_ref, out_ref):
    parts = [own_ref[:, lane * LANES : (lane + 1) * LANES] for lane in range(BLOCK // LANES)]
    stats = jnp.concatenate(parts, axis=0).astype(bf16)
    for block in range(BLOCKS):
        for lane in range(QUADS):
            total = mine_ref[block, lane] + other_ref[block, lane].astype(f32)
            out_ref[block * QUADS + lane, :HALF] = total.astype(bf16)
            out_ref[block * QUADS + lane, HALF:] = stats


def sent_groups(row_block):
    near = [(side, (row_block + step) % 4) for side in range(2) for step in range(2)]
    return near + [(row_block // 2, (row_block + 2) % 4)]


def picked(terms_ref, slot, chip):
    rows = terms_ref[chip, HALF:].astype(f32)
    for number in range(1, ROOTS):
        rows = jnp.where(slot == number, terms_ref[number * PAIR + chip, HALF:].astype(f32), rows)
    return rows


def reduce_kernel(owners_ref, terms_ref, out_ref):
    block = near_place(this_device())[0]
    row_block = this_device() % SHARDS // 16
    lanes = []
    for side in range(2):
        slot = owners_ref[pl.ds(side * BLOCKS + block, 1)]
        low, high = (picked(terms_ref, slot, chip) for chip in range(PAIR))
        rows = [slice(lane * OWN_ROWS, (lane + 1) * OWN_ROWS) for lane in range(4)]
        lanes.append([jnp.concatenate([low[place], high[place]], axis=0) for place in rows])
    stats = []
    for group in range(GROUPS):
        chosen = None
        for number in range(4):
            side, lane = sent_groups(number)[group]
            here = lanes[side][lane]
            chosen = here if chosen is None else jnp.where(row_block == number, here, chosen)
        stats.append(chosen.astype(bf16))
    for part in range(FAR):
        rows = slice(part * TILE, (part + 1) * TILE)
        total = terms_ref[0, rows].astype(f32)
        for source in range(1, XS * QUADS):
            total += terms_ref[source, rows].astype(f32)
        out_ref[part, :TILE] = total.astype(bf16)
        for group in range(GROUPS):
            out_ref[part, TILE * (group + 1) : TILE * (group + 2)] = stats[group]


def total_kernel(parts_ref, gradient_ref):
    total = parts_ref[0, :TILE].astype(f32)
    for part in range(1, FAR):
        total += parts_ref[part, :TILE].astype(f32)
    gradient = total.astype(bf16)
    for part in range(PARTS):
        gradient_ref[part] = gradient


def unpack_kernel(parts_here_ref, parts_there_ref, stats):
    core = this_device() % CORES
    for parts_ref, at in ((parts_here_ref, core), (parts_there_ref, 1 - core)):
        for part in range(FAR):
            row_block, column = divmod(part, 4)
            for group, (side, lane) in enumerate(sent_groups(row_block)):
                value = parts_ref[part, TILE * (group + 1) : TILE * (group + 2)].astype(f32)
                for low in range(PAIR):
                    shard = (row_block * PAIR + low) * 8 + column * CORES + at
                    place = pl.ds(pl.multiple_of(shard * OWN_ROWS, OWN_ROWS), OWN_ROWS)
                    columns = slice(lane * LANES, (lane + 1) * LANES)
                    stats[side, place, columns] = value[low * OWN_ROWS : (low + 1) * OWN_ROWS]
    for row_block in range(4):
        for side, lane in sent_groups(row_block):
            if lane != row_block:
                rows = slice(row_block * LANES, (row_block + 1) * LANES)
                columns = slice(lane * LANES, (lane + 1) * LANES)
                stats[side, columns, rows] = stats[side, rows, columns].T


def product(left, right):
    return jnp.dot(left.astype(bf16), right.astype(bf16), preferred_element_type=f32)


def symmetric(left, right, dims=((1,), (0,))):
    left, right = left[...].astype(bf16), right[...].astype(bf16)
    (left_dim,), (right_dim,) = dims

    def part(rows, columns):
        first = left[rows] if left_dim == 1 else left[:, rows]
        second = right[:, columns] if right_dim == 0 else right[columns]
        return lax.dot_general(first, second, (dims, ((), ())), preferred_element_type=f32)

    low, high = slice(0, HALF), slice(HALF, BLOCK)
    top = part(low, slice(0, BLOCK))
    corner = part(high, high)
    return jnp.concatenate([top, jnp.concatenate([top[:, HALF:].T, corner], axis=1)], axis=0)


def newton(stats, gram):
    sides = range(2)
    updated = [ema_decay * stats[side] + (1.0 - ema_decay) * gram[side] for side in sides]
    scales = [jnp.sqrt(jnp.sum(value * value, keepdims=True) + 1e-06) for value in updated]

    def step(state):
        low = [2.0 * state[side] - symmetric(state[side], state[side]) for side in sides]
        high = [2.0 * low[side] - symmetric(low[side], low[side]) for side in sides]
        return [1.25**4 * (state[side] - symmetric(high[side], state[side])) for side in sides]

    first = [updated[side] * (0.2 / scales[side]) for side in sides]
    second = step(first)
    return first, second, step(second)


def root_rows(first, second, third, diagonal, times=product):
    own_first, own_second, own_third = first
    both = own_first + own_second - times(own_first, second)
    return 1.25**3 * (diagonal - (both + own_third - times(both, third)))


def root_kernel(
    owners_ref,
    stats,
    tiles_here_ref,
    tiles_there_ref,
    out_ref,
    grad,
    gram,
    rows,
):
    device = this_device()
    position = device % SHARDS
    block, near_y, _, core = near_place(device)
    for tiles_ref, at in ((tiles_here_ref, core), (tiles_there_ref, 1 - core)):
        for part in range(PARTS):
            lane, group = divmod(part, FAR)
            place = pl.ds(pl.multiple_of(at * HALF + group * TILE, TILE), TILE)
            grad[place, lane * LANES : (lane + 1) * LANES] = tiles_ref[part]
    gram[0] = symmetric(grad, grad, ((1,), (1,)))
    gram[1] = symmetric(grad, grad, ((0,), (0,)))
    own = pl.ds(pl.multiple_of(position * OWN_ROWS, OWN_ROWS), OWN_ROWS)
    sides = [gram[side, own, :] for side in range(2)]
    for receiver in range(XS):
        held = held_by(receiver * PAIR + near_y, owners_ref)
        for lane in range(BLOCK // LANES):
            columns = slice(lane * LANES, (lane + 1) * LANES)
            rows_out = jnp.where(held == block, sides[0][:, columns], 0.0)
            rows_out = jnp.where(held == block + BLOCKS, sides[1][:, columns], rows_out)
            out_ref[receiver, OUT_ROWS:, columns] = rows_out

    start = pl.multiple_of(position % (BLOCK // OUT_ROWS) * OUT_ROWS, OUT_ROWS)
    states = newton(stats, gram)
    left, right = [[state[side] for state in states] for side in range(2)]
    for number in range(3):
        rows[number] = left[number]
    own = tuple(rows[number, pl.ds(start, OUT_ROWS), :] for number in range(3))
    shape = (OUT_ROWS, BLOCK)
    diagonal = lax.broadcasted_iota(jnp.int32, shape, 0) + start == lax.broadcasted_iota(jnp.int32, shape, 1)
    left_rows = root_rows(own, left[1], left[2], jnp.where(diagonal, 1.0, 0.0)).astype(bf16)
    mixed = jnp.dot(left_rows, grad[...], preferred_element_type=f32).astype(bf16)

    shape = (BLOCK, BLOCK)
    diagonal = lax.broadcasted_iota(jnp.int32, shape, 0) == lax.broadcasted_iota(jnp.int32, shape, 1)
    right_root = root_rows(
        right, right[1], right[2], jnp.where(diagonal, 1.0, 0.0), symmetric
    ).astype(bf16)
    piece = jnp.dot(mixed, right_root, preferred_element_type=f32)
    for receiver in range(XS):
        out_ref[receiver, :OUT_ROWS] = piece


def join_kernel(own_ref, pieces_ref, updated_ref, direction_ref):
    rows = pieces_ref[0, OUT_ROWS:]
    for source in range(1, XS):
        rows += pieces_ref[source, OUT_ROWS:]
    updated_ref[...] = ema_decay * own_ref[...] + (1.0 - ema_decay) * rows
    first = this_device() % SHARDS // (BLOCK // OUT_ROWS) * COLS
    for col in range(COLS):
        direction_ref[:, col * BLOCK : (col + 1) * BLOCK] = pieces_ref[first + col, :OUT_ROWS]


def exchange(value, axes):
    return lax.all_to_all(value, axes, split_axis=0, concat_axis=0, tiled=True)


def call(kernel, name, outs, arrays, scratch=(), limit=VMEM_LIMIT):
    vmem = pl.BlockSpec(memory_space=pltpu.VMEM)
    smem = pl.BlockSpec(memory_space=pltpu.SMEM)
    rest = pl.BlockSpec(memory_space=pl.ANY) if limit > VMEM_LIMIT else vmem
    return pl.pallas_call(
        kernel,
        out_shape=outs,
        in_specs=[smem if array.ndim == 1 else rest for array in arrays],
        out_specs=tuple(rest for _ in outs) if isinstance(outs, tuple) else rest,
        scratch_shapes=list(scratch),
        compiler_params=pltpu.CompilerParams(vmem_limit_bytes=limit),
        name=name,
    )(*arrays)


def swap(value, axis):
    return lax.ppermute(value, axis, [(0, 1), (1, 0)])


def body(activations, cotangents, statistics, owner):
    array = jax.ShapeDtypeStruct
    own = statistics[0]
    tokens = activations.shape[0]

    other = call(
        theirs_kernel,
        "grad_theirs",
        array((BLOCKS, QUADS, HALF, LANES), bf16),
        (activations, cotangents),
        scratch=[
            pltpu.VMEM((2, tokens, HALF), bf16),
            pltpu.VMEM((COLS, tokens, BLOCK), bf16),
            pltpu.VMEM((BLOCKS, QUADS, HALF, LANES), bf16),
            pltpu.SemaphoreType.DMA((4,)),
            pltpu.SemaphoreType.DMA((BLOCKS,)),
        ],
        limit=GRAD_LIMIT,
    )
    mine, owners = call(
        mine_kernel,
        "grad_mine",
        (array((BLOCKS, QUADS, HALF, LANES), f32), array((ROOTS, LANES), jnp.int32)),
        (owner, activations, cotangents),
    )
    packed = call(
        pack_kernel,
        "pack",
        array((XS * QUADS, HALF + STATS, LANES), bf16),
        (mine, swap(other, "core"), own),
    )
    reduced = call(
        reduce_kernel,
        "reduce",
        array((FAR, TILE * (1 + GROUPS), LANES), bf16),
        (owners, exchange(packed, NEAR_AXES)),
    )
    parts = exchange(reduced, FAR_AXES)
    gradient = call(total_kernel, "total", array((PARTS, TILE, LANES), bf16), (parts,))
    rows = call(
        unpack_kernel, "unpack", array((2, BLOCK, BLOCK), f32), (parts, swap(parts, "core"))
    )
    tiles = exchange(gradient, PLANE)
    pieces = call(
        root_kernel,
        "root",
        array((XS, OUT_ROWS + OWN_ROWS, BLOCK), f32),
        (owners, rows, tiles, swap(tiles, "core")),
        scratch=[
            pltpu.VMEM((BLOCK, BLOCK), bf16),
            pltpu.VMEM((2, BLOCK, BLOCK), f32),
            pltpu.VMEM((3, BLOCK, BLOCK), f32),
        ],
    )
    updated, direction = call(
        join_kernel,
        "join",
        (array((OWN_ROWS, BLOCK), f32), array((OUT_ROWS, COLS * BLOCK), f32)),
        (own, exchange(pieces, "x")),
    )
    return updated[None], direction


def solution(mesh):
    sizes = {"x": 4, "yl": 2, "z4": 4, "zp": 2, "yh": 4, "core": 2}
    fine = Mesh(mesh.devices.reshape(tuple(sizes.values())), tuple(sizes))
    every = tuple(sizes)
    rep, shard = every[:2], every[2:]
    return jax.shard_map(
        body,
        mesh=fine,
        in_specs=(P(every, None), P(every, None), P(rep, shard, None), P()),
        out_specs=(P(rep, shard, None), P(shard, None)),
        check_vma=False,
    )
```

```python
import jax
import jax.numpy as jnp
from jax import lax
from jax.experimental import pallas as pl
from jax.experimental.pallas import tpu as pltpu
from jax.sharding import Mesh
from jax.sharding import PartitionSpec as P

ema_decay = 0.9
BLOCK = 512
HALF = BLOCK // 2
LANES = 128
BLOCKS = 4
ROOTS = 8
COLS = 2
XS = 4
PAIR = 2
CORES = 2
SHARDS = 64
QUADS = 4
FAR = 16
PARTS = QUADS * FAR
OUT_ROWS = 16
OWN_ROWS = 8
STATS = 32
GROUPS = 5
TILE = 16
f32 = jnp.float32
bf16 = jnp.bfloat16
NEAR_AXES = ("x", "yl", "zp")
FAR_AXES = ("z4", "yh")
PLANE = ("yl", "zp") + FAR_AXES
DEVICE_AXES = ("x", "yl", "z4", "zp", "yh", "core")
VMEM_LIMIT = 40 * 1024 * 1024
GRAD_LIMIT = 60 * 1024 * 1024


def held_by(slot, owners_ref):
    held = jnp.zeros((1, LANES), jnp.int32)
    for root in range(1, ROOTS):
        held = jnp.where(owners_ref[root : root + 1] == slot, root, held)
    return held


def this_device():
    return lax.axis_index(DEVICE_AXES)


def near_place(device):
    return device // (PAIR * SHARDS), device // SHARDS % PAIR, device // 8 % PAIR, device % CORES


def theirs_kernel(act_hbm, cot_hbm, out_hbm, act_ref, cot_ref, out_ref, sems, out_sems):
    half = 1 - this_device() % CORES
    copies = []
    for row in range(2):
        start = pl.multiple_of(row * BLOCK + half * HALF, HALF)
        copies.append(
            pltpu.make_async_copy(act_hbm.at[:, pl.ds(start, HALF)], act_ref.at[row], sems.at[row])
        )
    for col in range(COLS):
        columns = pl.ds(col * BLOCK, BLOCK)
        copies.append(
            pltpu.make_async_copy(cot_hbm.at[:, columns], cot_ref.at[col], sems.at[2 + col])
        )
    for number in (0, 2, 3, 1):
        copies[number].start()
    sent = []
    for row in range(2):
        copies[row].wait()
        for col in range(COLS):
            if row == 0:
                copies[2 + col].wait()
            block = row * COLS + col
            term = half_term(act_ref[row], cot_ref[col]).astype(bf16)
            for lane in range(QUADS):
                out_ref[block, lane] = term[:, lane * LANES : (lane + 1) * LANES]
            sent.append(
                pltpu.make_async_copy(out_ref.at[block], out_hbm.at[block], out_sems.at[block])
            )
            sent[-1].start()
    for copy in sent:
        copy.wait()


def half_term(act, cot):
    return lax.dot_general(act, cot, (((0,), (0,)), ((), ())), preferred_element_type=f32)


def mine_kernel(owner_ref, act_ref, cot_ref, out_ref, owners_ref):
    for root in range(ROOTS):
        owners_ref[root : root + 1] = jnp.full((1, LANES), owner_ref[root], jnp.int32)
    half = this_device() % CORES
    for row in range(2):
        start = pl.multiple_of(row * BLOCK + half * HALF, HALF)
        act = act_ref[:, pl.ds(start, HALF)]
        for col in range(COLS):
            term = half_term(act, cot_ref[:, col * BLOCK : (col + 1) * BLOCK])
            for lane in range(QUADS):
                out_ref[row * COLS + col, lane] = term[:, lane * LANES : (lane + 1) * LANES]


def pack_kernel(mine_ref, other_ref, own_ref, out_ref):
    parts = [own_ref[:, lane * LANES : (lane + 1) * LANES] for lane in range(BLOCK // LANES)]
    stats = jnp.concatenate(parts, axis=0).astype(bf16)
    for block in range(BLOCKS):
        for lane in range(QUADS):
            total = mine_ref[block, lane] + other_ref[block, lane].astype(f32)
            out_ref[block * QUADS + lane, :HALF] = total.astype(bf16)
            out_ref[block * QUADS + lane, HALF:] = stats


def sent_groups(row_block):
    near = [(side, (row_block + step) % 4) for side in range(2) for step in range(2)]
    return near + [(row_block // 2, (row_block + 2) % 4)]


def picked(terms_ref, slot, chip):
    rows = terms_ref[chip, HALF:].astype(f32)
    for number in range(1, ROOTS):
        rows = jnp.where(slot == number, terms_ref[number * PAIR + chip, HALF:].astype(f32), rows)
    return rows


def reduce_kernel(owners_ref, terms_ref, out_ref):
    block = near_place(this_device())[0]
    row_block = this_device() % SHARDS // 16
    lanes = []
    for side in range(2):
        slot = owners_ref[pl.ds(side * BLOCKS + block, 1)]
        low, high = (picked(terms_ref, slot, chip) for chip in range(PAIR))
        rows = [slice(lane * OWN_ROWS, (lane + 1) * OWN_ROWS) for lane in range(4)]
        lanes.append([jnp.concatenate([low[place], high[place]], axis=0) for place in rows])
    stats = []
    for group in range(GROUPS):
        chosen = None
        for number in range(4):
            side, lane = sent_groups(number)[group]
            here = lanes[side][lane]
            chosen = here if chosen is None else jnp.where(row_block == number, here, chosen)
        stats.append(chosen.astype(bf16))
    for part in range(FAR):
        rows = slice(part * TILE, (part + 1) * TILE)
        total = terms_ref[0, rows].astype(f32)
        for source in range(1, XS * QUADS):
            total += terms_ref[source, rows].astype(f32)
        out_ref[part, :TILE] = total.astype(bf16)
        for group in range(GROUPS):
            out_ref[part, TILE * (group + 1) : TILE * (group + 2)] = stats[group]


def total_kernel(parts_ref, gradient_hbm, copies_ref, sems):
    total = parts_ref[0, :TILE].astype(f32)
    for part in range(1, FAR):
        total += parts_ref[part, :TILE].astype(f32)
    gradient = total.astype(bf16)
    for part in range(FAR):
        copies_ref[part] = gradient
    sent = []
    for quad in range(QUADS):
        place = pl.ds(quad * FAR, FAR)
        sent.append(pltpu.make_async_copy(copies_ref, gradient_hbm.at[place], sems.at[quad]))
        sent[-1].start()
    for copy in sent:
        copy.wait()


def unpack_kernel(parts_here_ref, parts_there_ref, stats):
    core = this_device() % CORES
    for parts_ref, at in ((parts_here_ref, core), (parts_there_ref, 1 - core)):
        for part in range(FAR):
            row_block, column = divmod(part, 4)
            for group, (side, lane) in enumerate(sent_groups(row_block)):
                value = parts_ref[part, TILE * (group + 1) : TILE * (group + 2)].astype(f32)
                value = ema_decay * value
                for low in range(PAIR):
                    shard = (row_block * PAIR + low) * 8 + column * CORES + at
                    place = pl.ds(pl.multiple_of(shard * OWN_ROWS, OWN_ROWS), OWN_ROWS)
                    columns = slice(lane * LANES, (lane + 1) * LANES)
                    stats[side, place, columns] = value[low * OWN_ROWS : (low + 1) * OWN_ROWS]
    for row_block in range(4):
        for side, lane in sent_groups(row_block):
            if lane != row_block:
                rows = slice(row_block * LANES, (row_block + 1) * LANES)
                columns = slice(lane * LANES, (lane + 1) * LANES)
                stats[side, columns, rows] = stats[side, rows, columns].T


def product(left, right):
    return jnp.dot(left.astype(bf16), right.astype(bf16), preferred_element_type=f32)


def symmetric(left, right, dims=((1,), (0,))):
    left, right = left[...].astype(bf16), right[...].astype(bf16)
    (left_dim,), (right_dim,) = dims

    def part(rows, columns):
        first = left[rows] if left_dim == 1 else left[:, rows]
        second = right[:, columns] if right_dim == 0 else right[columns]
        return lax.dot_general(first, second, (dims, ((), ())), preferred_element_type=f32)

    low, high = slice(0, HALF), slice(HALF, BLOCK)
    top = part(low, slice(0, BLOCK))
    corner = part(high, high)
    return jnp.concatenate([top, jnp.concatenate([top[:, HALF:].T, corner], axis=1)], axis=0)


def newton(stats, gram):
    sides = range(2)
    updated = [stats[side] + (1.0 - ema_decay) * gram[side] for side in sides]
    scales = [jnp.sqrt(jnp.sum(value * value, keepdims=True) + 1e-06) for value in updated]

    def step(state):
        low = [2.0 * state[side] - symmetric(state[side], state[side]) for side in sides]
        high = [2.0 * low[side] - symmetric(low[side], low[side]) for side in sides]
        return [1.25**4 * (state[side] - symmetric(high[side], state[side])) for side in sides]

    first = [updated[side] * (0.2 / scales[side]) for side in sides]
    second = step(first)
    return first, second, step(second)


def root_rows(first, second, third, diagonal, times=product):
    own_first, own_second, own_third = first
    both = own_first + own_second - times(own_first, second)
    return 1.25**3 * (diagonal - (both + own_third - times(both, third)))


def root_kernel(
    owners_ref,
    stats,
    tiles_here_ref,
    tiles_there_ref,
    out_ref,
    grad,
    gram,
    rows,
):
    device = this_device()
    position = device % SHARDS
    block, near_y, _, core = near_place(device)
    for tiles_ref, at in ((tiles_here_ref, core), (tiles_there_ref, 1 - core)):
        for part in range(PARTS):
            lane, group = divmod(part, FAR)
            place = pl.ds(pl.multiple_of(at * HALF + group * TILE, TILE), TILE)
            grad[place, lane * LANES : (lane + 1) * LANES] = tiles_ref[part]
    gram[0] = symmetric(grad, grad, ((1,), (1,)))
    gram[1] = symmetric(grad, grad, ((0,), (0,)))
    own = pl.ds(pl.multiple_of(position * OWN_ROWS, OWN_ROWS), OWN_ROWS)
    sides = [gram[side, own, :] for side in range(2)]
    for receiver in range(XS):
        held = held_by(receiver * PAIR + near_y, owners_ref)
        for lane in range(BLOCK // LANES):
            columns = slice(lane * LANES, (lane + 1) * LANES)
            rows_out = jnp.where(held == block, sides[0][:, columns], 0.0)
            rows_out = jnp.where(held == block + BLOCKS, sides[1][:, columns], rows_out)
            out_ref[receiver, OUT_ROWS:, columns] = rows_out

    start = pl.multiple_of(position % (BLOCK // OUT_ROWS) * OUT_ROWS, OUT_ROWS)
    states = newton(stats, gram)
    left, right = [[state[side] for state in states] for side in range(2)]
    shape = (BLOCK, BLOCK)
    diagonal = lax.broadcasted_iota(jnp.int32, shape, 0) == lax.broadcasted_iota(jnp.int32, shape, 1)
    right_root = root_rows(
        right, right[1], right[2], jnp.where(diagonal, 1.0, 0.0), symmetric
    ).astype(bf16)
    for number in range(3):
        rows[number] = left[number]
    own = tuple(rows[number, pl.ds(start, OUT_ROWS), :] for number in range(3))
    shape = (OUT_ROWS, BLOCK)
    diagonal = lax.broadcasted_iota(jnp.int32, shape, 0) + start == lax.broadcasted_iota(jnp.int32, shape, 1)
    left_rows = root_rows(own, left[1], left[2], jnp.where(diagonal, 1.0, 0.0)).astype(bf16)
    mixed = jnp.dot(left_rows, grad[...], preferred_element_type=f32).astype(bf16)

    piece = jnp.dot(mixed, right_root, preferred_element_type=f32)
    for receiver in range(XS):
        out_ref[receiver, :OUT_ROWS] = piece


def join_kernel(own_ref, pieces_ref, updated_ref, direction_ref):
    rows = pieces_ref[0, OUT_ROWS:]
    for source in range(1, XS):
        rows += pieces_ref[source, OUT_ROWS:]
    updated_ref[...] = ema_decay * own_ref[...] + (1.0 - ema_decay) * rows
    first = this_device() % SHARDS // (BLOCK // OUT_ROWS) * COLS
    for col in range(COLS):
        direction_ref[:, col * BLOCK : (col + 1) * BLOCK] = pieces_ref[first + col, :OUT_ROWS]


def exchange(value, axes):
    return lax.all_to_all(value, axes, split_axis=0, concat_axis=0, tiled=True)


vmem = pl.BlockSpec(memory_space=pltpu.VMEM)
smem = pl.BlockSpec(memory_space=pltpu.SMEM)
anywhere = pl.BlockSpec(memory_space=pl.ANY)


def call(kernel, name, outs, arrays, scratch=(), limit=VMEM_LIMIT, operands=vmem, results=vmem):
    return pl.pallas_call(
        kernel,
        out_shape=outs,
        in_specs=[smem if array.ndim == 1 else operands for array in arrays],
        out_specs=tuple(results for _ in outs) if isinstance(outs, tuple) else results,
        scratch_shapes=list(scratch),
        compiler_params=pltpu.CompilerParams(vmem_limit_bytes=limit),
        name=name,
    )(*arrays)


def swap(value, axis):
    return lax.ppermute(value, axis, [(0, 1), (1, 0)])


def body(activations, cotangents, statistics, owner):
    array = jax.ShapeDtypeStruct
    own = statistics[0]
    tokens = activations.shape[0]

    other = call(
        theirs_kernel,
        "grad_theirs",
        array((BLOCKS, QUADS, HALF, LANES), bf16),
        (activations, cotangents),
        scratch=[
            pltpu.VMEM((2, tokens, HALF), bf16),
            pltpu.VMEM((COLS, tokens, BLOCK), bf16),
            pltpu.VMEM((BLOCKS, QUADS, HALF, LANES), bf16),
            pltpu.SemaphoreType.DMA((4,)),
            pltpu.SemaphoreType.DMA((BLOCKS,)),
        ],
        limit=GRAD_LIMIT,
        operands=anywhere,
        results=anywhere,
    )
    mine, owners = call(
        mine_kernel,
        "grad_mine",
        (array((BLOCKS, QUADS, HALF, LANES), f32), array((ROOTS, LANES), jnp.int32)),
        (owner, activations, cotangents),
    )
    packed = call(
        pack_kernel,
        "pack",
        array((XS * QUADS, HALF + STATS, LANES), bf16),
        (mine, swap(other, "core"), own),
    )
    reduced = call(
        reduce_kernel,
        "reduce",
        array((FAR, TILE * (1 + GROUPS), LANES), bf16),
        (owners, exchange(packed, NEAR_AXES)),
    )
    parts = exchange(reduced, FAR_AXES)
    gradient = call(
        total_kernel,
        "total",
        array((PARTS, TILE, LANES), bf16),
        (parts,),
        scratch=[pltpu.VMEM((FAR, TILE, LANES), bf16), pltpu.SemaphoreType.DMA((QUADS,))],
        results=anywhere,
    )
    rows = call(
        unpack_kernel, "unpack", array((2, BLOCK, BLOCK), f32), (parts, swap(parts, "core"))
    )
    tiles = exchange(gradient, PLANE)
    pieces = call(
        root_kernel,
        "root",
        array((XS, OUT_ROWS + OWN_ROWS, BLOCK), f32),
        (owners, rows, tiles, swap(tiles, "core")),
        scratch=[
            pltpu.VMEM((BLOCK, BLOCK), bf16),
            pltpu.VMEM((2, BLOCK, BLOCK), f32),
            pltpu.VMEM((3, BLOCK, BLOCK), f32),
        ],
    )
    updated, direction = call(
        join_kernel,
        "join",
        (array((OWN_ROWS, BLOCK), f32), array((OUT_ROWS, COLS * BLOCK), f32)),
        (own, exchange(pieces, "x")),
    )
    return updated[None], direction


def solution(mesh):
    sizes = {"x": 4, "yl": 2, "z4": 4, "zp": 2, "yh": 4, "core": 2}
    fine = Mesh(mesh.devices.reshape(tuple(sizes.values())), tuple(sizes))
    every = tuple(sizes)
    rep, shard = every[:2], every[2:]
    return jax.shard_map(
        body,
        mesh=fine,
        in_specs=(P(every, None), P(every, None), P(rep, shard, None), P()),
        out_specs=(P(rep, shard, None), P(shard, None)),
        check_vma=False,
    )
```

```python
import jax
import jax.numpy as jnp
from jax import lax
from jax.experimental import pallas as pl
from jax.experimental.pallas import tpu as pltpu
from jax.sharding import Mesh
from jax.sharding import PartitionSpec as P

ema_decay = 0.9
BLOCK = 512
HALF = BLOCK // 2
LANES = 128
BLOCKS = 4
ROOTS = 8
COLS = 2
XS = 4
PAIR = 2
CORES = 2
SHARDS = 64
QUADS = 4
FAR = 16
PARTS = QUADS * FAR
OUT_ROWS = 16
OWN_ROWS = 8
STATS = 32
GROUPS = 5
TILE = 16
f32 = jnp.float32
bf16 = jnp.bfloat16
NEAR_AXES = ("x", "yl", "zp")
FAR_AXES = ("z4", "yh")
PLANE = ("yl", "zp") + FAR_AXES
DEVICE_AXES = ("x", "yl", "z4", "zp", "yh", "core")
VMEM_LIMIT = 40 * 1024 * 1024
GRAD_LIMIT = 60 * 1024 * 1024


def held_by(slot, owners_ref):
    held = jnp.zeros((1, LANES), jnp.int32)
    for root in range(1, ROOTS):
        held = jnp.where(owners_ref[root : root + 1] == slot, root, held)
    return held


def this_device():
    return lax.axis_index(DEVICE_AXES)


def near_place(device):
    return device // (PAIR * SHARDS), device // SHARDS % PAIR, device // 8 % PAIR, device % CORES


def theirs_kernel(act_hbm, cot_hbm, out_hbm, act_ref, cot_ref, out_ref, sems, out_sems):
    half = 1 - this_device() % CORES
    copies = []
    for row in range(2):
        start = pl.multiple_of(row * BLOCK + half * HALF, HALF)
        copies.append(
            pltpu.make_async_copy(act_hbm.at[:, pl.ds(start, HALF)], act_ref.at[row], sems.at[row])
        )
    for col in range(COLS):
        columns = pl.ds(col * BLOCK, BLOCK)
        copies.append(
            pltpu.make_async_copy(cot_hbm.at[:, columns], cot_ref.at[col], sems.at[2 + col])
        )
    for number in (0, 2, 3, 1):
        copies[number].start()
    sent = []
    for row in range(2):
        copies[row].wait()
        for col in range(COLS):
            if row == 0:
                copies[2 + col].wait()
            block = row * COLS + col
            term = half_term(act_ref[row], cot_ref[col]).astype(bf16)
            for lane in range(QUADS):
                out_ref[block, lane] = term[:, lane * LANES : (lane + 1) * LANES]
            sent.append(
                pltpu.make_async_copy(out_ref.at[block], out_hbm.at[block], out_sems.at[block])
            )
            sent[-1].start()
    for copy in sent:
        copy.wait()


def half_term(act, cot):
    return lax.dot_general(act, cot, (((0,), (0,)), ((), ())), preferred_element_type=f32)


def mine_kernel(owner_ref, act_ref, cot_ref, out_ref, owners_ref):
    for root in range(ROOTS):
        owners_ref[root : root + 1] = jnp.full((1, LANES), owner_ref[root], jnp.int32)
    half = this_device() % CORES
    for row in range(2):
        start = pl.multiple_of(row * BLOCK + half * HALF, HALF)
        act = act_ref[:, pl.ds(start, HALF)]
        for col in range(COLS):
            term = half_term(act, cot_ref[:, col * BLOCK : (col + 1) * BLOCK])
            for lane in range(QUADS):
                out_ref[row * COLS + col, lane] = term[:, lane * LANES : (lane + 1) * LANES]


def pack_kernel(mine_ref, other_ref, own_ref, out_ref):
    parts = [own_ref[:, lane * LANES : (lane + 1) * LANES] for lane in range(BLOCK // LANES)]
    stats = jnp.concatenate(parts, axis=0).astype(bf16)
    for block in range(BLOCKS):
        for lane in range(QUADS):
            total = mine_ref[block, lane] + other_ref[block, lane].astype(f32)
            out_ref[block * QUADS + lane, :HALF] = total.astype(bf16)
            out_ref[block * QUADS + lane, HALF:] = stats


def sent_groups(row_block):
    near = [(side, (row_block + step) % 4) for side in range(2) for step in range(2)]
    return near + [(row_block // 2, (row_block + 2) % 4)]


def picked(terms_ref, slot, chip):
    rows = terms_ref[chip, HALF:].astype(f32)
    for number in range(1, ROOTS):
        rows = jnp.where(slot == number, terms_ref[number * PAIR + chip, HALF:].astype(f32), rows)
    return rows


def reduce_kernel(owners_ref, terms_ref, out_ref):
    block = near_place(this_device())[0]
    row_block = this_device() % SHARDS // 16
    lanes = []
    for side in range(2):
        slot = owners_ref[pl.ds(side * BLOCKS + block, 1)]
        low, high = (picked(terms_ref, slot, chip) for chip in range(PAIR))
        rows = [slice(lane * OWN_ROWS, (lane + 1) * OWN_ROWS) for lane in range(4)]
        lanes.append([jnp.concatenate([low[place], high[place]], axis=0) for place in rows])
    stats = []
    for group in range(GROUPS):
        chosen = None
        for number in range(4):
            side, lane = sent_groups(number)[group]
            here = lanes[side][lane]
            chosen = here if chosen is None else jnp.where(row_block == number, here, chosen)
        stats.append(chosen.astype(bf16))
    for part in range(FAR):
        rows = slice(part * TILE, (part + 1) * TILE)
        total = terms_ref[0, rows].astype(f32)
        for source in range(1, XS * QUADS):
            total += terms_ref[source, rows].astype(f32)
        out_ref[part, :TILE] = total.astype(bf16)
        for group in range(GROUPS):
            out_ref[part, TILE * (group + 1) : TILE * (group + 2)] = stats[group]


def total_kernel(parts_ref, gradient_ref):
    total = parts_ref[0, :TILE].astype(f32)
    for part in range(1, FAR):
        total += parts_ref[part, :TILE].astype(f32)
    gradient = total.astype(bf16)
    for part in range(PARTS):
        gradient_ref[part] = gradient


def unpack_kernel(parts_here_ref, parts_there_ref, stats):
    core = this_device() % CORES
    for parts_ref, at in ((parts_here_ref, core), (parts_there_ref, 1 - core)):
        for part in range(FAR):
            row_block, column = divmod(part, 4)
            for group, (side, lane) in enumerate(sent_groups(row_block)):
                value = parts_ref[part, TILE * (group + 1) : TILE * (group + 2)].astype(f32)
                value = ema_decay * value
                for low in range(PAIR):
                    shard = (row_block * PAIR + low) * 8 + column * CORES + at
                    place = pl.ds(pl.multiple_of(shard * OWN_ROWS, OWN_ROWS), OWN_ROWS)
                    columns = slice(lane * LANES, (lane + 1) * LANES)
                    stats[side, place, columns] = value[low * OWN_ROWS : (low + 1) * OWN_ROWS]
    for row_block in range(4):
        for side, lane in sent_groups(row_block):
            if lane != row_block:
                rows = slice(row_block * LANES, (row_block + 1) * LANES)
                columns = slice(lane * LANES, (lane + 1) * LANES)
                stats[side, columns, rows] = stats[side, rows, columns].T


def product(left, right):
    return jnp.dot(left.astype(bf16), right.astype(bf16), preferred_element_type=f32)


def symmetric(left, right, dims=((1,), (0,))):
    left, right = left[...].astype(bf16), right[...].astype(bf16)
    (left_dim,), (right_dim,) = dims

    def part(rows, columns):
        first = left[rows] if left_dim == 1 else left[:, rows]
        second = right[:, columns] if right_dim == 0 else right[columns]
        return lax.dot_general(first, second, (dims, ((), ())), preferred_element_type=f32)

    low, high = slice(0, HALF), slice(HALF, BLOCK)
    top = part(low, slice(0, BLOCK))
    corner = part(high, high)
    return jnp.concatenate([top, jnp.concatenate([top[:, HALF:].T, corner], axis=1)], axis=0)


def newton(stats, gram):
    sides = range(2)
    updated = [stats[side] + (1.0 - ema_decay) * gram[side] for side in sides]
    scales = [jnp.sqrt(jnp.sum(value * value, keepdims=True) + 1e-06) for value in updated]

    def step(state):
        low = [2.0 * state[side] - symmetric(state[side], state[side]) for side in sides]
        high = [2.0 * low[side] - symmetric(low[side], low[side]) for side in sides]
        return [1.25**4 * (state[side] - symmetric(high[side], state[side])) for side in sides]

    first = [updated[side] * (0.2 / scales[side]) for side in sides]
    second = step(first)
    return first, second, step(second)


def root_rows(first, second, third, diagonal, times=product):
    own_first, own_second, own_third = first
    both = own_first + own_second - times(own_first, second)
    return 1.25**3 * (diagonal - (both + own_third - times(both, third)))


def root_kernel(
    owners_ref,
    stats,
    tiles_here_ref,
    tiles_there_ref,
    out_ref,
    grad,
    gram,
    rows,
):
    device = this_device()
    position = device % SHARDS
    block, near_y, _, core = near_place(device)
    for tiles_ref, at in ((tiles_here_ref, core), (tiles_there_ref, 1 - core)):
        for part in range(PARTS):
            lane, group = divmod(part, FAR)
            place = pl.ds(pl.multiple_of(at * HALF + group * TILE, TILE), TILE)
            grad[place, lane * LANES : (lane + 1) * LANES] = tiles_ref[part]
    gram[0] = symmetric(grad, grad, ((1,), (1,)))
    gram[1] = symmetric(grad, grad, ((0,), (0,)))
    own = pl.ds(pl.multiple_of(position * OWN_ROWS, OWN_ROWS), OWN_ROWS)
    sides = [gram[side, own, :] for side in range(2)]
    for receiver in range(XS):
        held = held_by(receiver * PAIR + near_y, owners_ref)
        for lane in range(BLOCK // LANES):
            columns = slice(lane * LANES, (lane + 1) * LANES)
            rows_out = jnp.where(held == block, sides[0][:, columns], 0.0)
            rows_out = jnp.where(held == block + BLOCKS, sides[1][:, columns], rows_out)
            out_ref[receiver, OUT_ROWS:, columns] = rows_out

    start = pl.multiple_of(position % (BLOCK // OUT_ROWS) * OUT_ROWS, OUT_ROWS)
    states = newton(stats, gram)
    left, right = [[state[side] for state in states] for side in range(2)]
    shape = (BLOCK, BLOCK)
    diagonal = lax.broadcasted_iota(jnp.int32, shape, 0) == lax.broadcasted_iota(jnp.int32, shape, 1)
    right_root = root_rows(
        right, right[1], right[2], jnp.where(diagonal, 1.0, 0.0), symmetric
    ).astype(bf16)
    for number in range(3):
        rows[number] = left[number]
    own = tuple(rows[number, pl.ds(start, OUT_ROWS), :] for number in range(3))
    shape = (OUT_ROWS, BLOCK)
    diagonal = lax.broadcasted_iota(jnp.int32, shape, 0) + start == lax.broadcasted_iota(jnp.int32, shape, 1)
    left_rows = root_rows(own, left[1], left[2], jnp.where(diagonal, 1.0, 0.0)).astype(bf16)
    mixed = jnp.dot(left_rows, grad[...], preferred_element_type=f32).astype(bf16)

    piece = jnp.dot(mixed, right_root, preferred_element_type=f32)
    for receiver in range(XS):
        out_ref[receiver, :OUT_ROWS] = piece


def join_kernel(own_ref, pieces_ref, updated_ref, direction_ref):
    rows = pieces_ref[0, OUT_ROWS:]
    for source in range(1, XS):
        rows += pieces_ref[source, OUT_ROWS:]
    updated_ref[...] = ema_decay * own_ref[...] + (1.0 - ema_decay) * rows
    first = this_device() % SHARDS // (BLOCK // OUT_ROWS) * COLS
    for col in range(COLS):
        direction_ref[:, col * BLOCK : (col + 1) * BLOCK] = pieces_ref[first + col, :OUT_ROWS]


def exchange(value, axes):
    return lax.all_to_all(value, axes, split_axis=0, concat_axis=0, tiled=True)


def call(kernel, name, outs, arrays, scratch=(), limit=VMEM_LIMIT):
    vmem = pl.BlockSpec(memory_space=pltpu.VMEM)
    smem = pl.BlockSpec(memory_space=pltpu.SMEM)
    rest = pl.BlockSpec(memory_space=pl.ANY) if limit > VMEM_LIMIT else vmem
    return pl.pallas_call(
        kernel,
        out_shape=outs,
        in_specs=[smem if array.ndim == 1 else rest for array in arrays],
        out_specs=tuple(rest for _ in outs) if isinstance(outs, tuple) else rest,
        scratch_shapes=list(scratch),
        compiler_params=pltpu.CompilerParams(vmem_limit_bytes=limit),
        name=name,
    )(*arrays)


def swap(value, axis):
    return lax.ppermute(value, axis, [(0, 1), (1, 0)])


def body(activations, cotangents, statistics, owner):
    array = jax.ShapeDtypeStruct
    own = statistics[0]
    tokens = activations.shape[0]

    other = call(
        theirs_kernel,
        "grad_theirs",
        array((BLOCKS, QUADS, HALF, LANES), bf16),
        (activations, cotangents),
        scratch=[
            pltpu.VMEM((2, tokens, HALF), bf16),
            pltpu.VMEM((COLS, tokens, BLOCK), bf16),
            pltpu.VMEM((BLOCKS, QUADS, HALF, LANES), bf16),
            pltpu.SemaphoreType.DMA((4,)),
            pltpu.SemaphoreType.DMA((BLOCKS,)),
        ],
        limit=GRAD_LIMIT,
    )
    mine, owners = call(
        mine_kernel,
        "grad_mine",
        (array((BLOCKS, QUADS, HALF, LANES), f32), array((ROOTS, LANES), jnp.int32)),
        (owner, activations, cotangents),
    )
    packed = call(
        pack_kernel,
        "pack",
        array((XS * QUADS, HALF + STATS, LANES), bf16),
        (mine, swap(other, "core"), own),
    )
    reduced = call(
        reduce_kernel,
        "reduce",
        array((FAR, TILE * (1 + GROUPS), LANES), bf16),
        (owners, exchange(packed, NEAR_AXES)),
    )
    parts = exchange(reduced, FAR_AXES)
    gradient = call(total_kernel, "total", array((PARTS, TILE, LANES), bf16), (parts,))
    rows = call(
        unpack_kernel, "unpack", array((2, BLOCK, BLOCK), f32), (parts, swap(parts, "core"))
    )
    tiles = exchange(gradient, PLANE)
    pieces = call(
        root_kernel,
        "root",
        array((XS, OUT_ROWS + OWN_ROWS, BLOCK), f32),
        (owners, rows, tiles, swap(tiles, "core")),
        scratch=[
            pltpu.VMEM((BLOCK, BLOCK), bf16),
            pltpu.VMEM((2, BLOCK, BLOCK), f32),
            pltpu.VMEM((3, BLOCK, BLOCK), f32),
        ],
    )
    updated, direction = call(
        join_kernel,
        "join",
        (array((OWN_ROWS, BLOCK), f32), array((OUT_ROWS, COLS * BLOCK), f32)),
        (own, exchange(pieces, "x")),
    )
    return updated[None], direction


def solution(mesh):
    sizes = {"x": 4, "yl": 2, "z4": 4, "zp": 2, "yh": 4, "core": 2}
    fine = Mesh(mesh.devices.reshape(tuple(sizes.values())), tuple(sizes))
    every = tuple(sizes)
    rep, shard = every[:2], every[2:]
    return jax.shard_map(
        body,
        mesh=fine,
        in_specs=(P(every, None), P(every, None), P(rep, shard, None), P()),
        out_specs=(P(rep, shard, None), P(shard, None)),
        check_vma=False,
    )
```
